256 devices in a mesh: gx: 4 (over x), gy: 8 (over y, core), gz: 8 (over z).
Axes of the slice: x: 4, y: 4, z: 8, core: 2. Of those that a mesh axis runs over, the one named last changes fastest.
Arguments:
- electrolyte: float32 [64, 128, 1024], P('gx', 'gy', 'gz'), may hold values from -6 to 6
- conductivity: float32 [64, 128, 1024], P('gx', 'gy', 'gz'), may hold values from 0.3 to 3
- phase_label: int32 [64, 128, 1024], P('gx', 'gy', 'gz'), may hold values 0 or 1
- applied_current: float32 [1], replicated, may hold values from 0.3 to 1
- slot_count: int32 [4, 8, 8], P('gx', 'gy', 'gz'), may hold values from 256 to 2048, as said below
- slot_cell: int32 [4, 8, 16384], P('gx', 'gy', 'gz'), may hold values from 0 to 32767, as said below
- slot_label: int32 [4, 8, 16384], P('gx', 'gy', 'gz'), may hold values from 0 to 1023
- slot_area: float32 [4, 8, 16384], P('gx', 'gy', 'gz'), may hold values from 0.5 to 2
- slot_rate: float32 [4, 8, 16384], P('gx', 'gy', 'gz'), may hold values from 0.3 to 3
- owner_map: int32 [4, 8, 1024], P('gx', 'gy'), may hold values from 0 to 1023, each once within a row
- shell_count: int32 [4, 8, 1024], P('gx', 'gy', 'gz'), may hold values from 8 to 64
- shell_conc: float32 [4, 8, 64, 1024], P('gx', 'gy', None, 'gz'), may hold values from 0.2 to 0.9
- shell_inverse: float32 [4, 8, 64, 64, 1024], P('gx', 'gy', None, None, 'gz'), as said below
Outputs:
- concentration: float32 [64, 128, 1024], P('gx', 'gy', 'gz')
- potential: float32 [64, 128, 1024], P('gx', 'gy', 'gz')
- shell_update: float32 [4, 8, 64, 1024], P('gx', 'gy', None, 'gz')
The draws below stay inside these ranges and needn't reach their ends.
Inputs may be any that keep to these rules, and one draw needn't show every extreme that they name: `slot_count`: the live counts rise along z from about a quarter of 2048 to 2048; in every draw some brick's list is full. `slot_cell`: the 2048 entries of one brick, padding included, name distinct voxels. `shell_inverse`: each row of each particle's matrix has a diagonal entry larger than the sum of the magnitudes of its other entries.
All inputs are finite; a program needn't handle non-finite values. No bound on the sum of `phase_label` on one device may be relied on, other than what follows from the above.
Results may differ from the reference program's by a relative error of at most 0.0001.
Values sent between devices are 32-bit elements; how exact they have to be, the bound alone decides.
No kernel may reach another device: no remote copies, remote signals or barrier semaphores. Data moves between devices by JAX's collectives and lax.ppermute only.
A program may use at most 128 MiB of HBM per device.

```python
import math
import jax
import jax.numpy as jnp
from jax import lax

CX = 16
CY = 16
CZ = 128
SLOTS = 2048
PART_DEV = 128
SHELLS = 64
SWEEPS = 2
ITERS = 8
NX = 64
NY = 128
NZ = 1024
COLUMN_PARTS = 1024
N_GX = 4
N_GY = 8
N_GZ = 8


def draw_slot_count(key, part):
    key = jax.random.fold_in(key, 11)
    jitter_key, chosen_key, lowest_key = jax.random.split(key, 3)
    layers = jnp.arange(N_GZ, dtype=jnp.int32)
    quarter = SLOTS // 4
    baseline = quarter + 3 * quarter * layers // max(N_GZ - 1, 1)
    jitter = jax.random.randint(jitter_key, (N_GX, N_GY, N_GZ), 0, SLOTS // 8 + 1)
    chosen = jax.random.randint(chosen_key, (), 0, N_GX * N_GY)
    lowest = jax.random.randint(lowest_key, (), 0, N_GX * N_GY)
    columns = jnp.arange(N_GX * N_GY, dtype=jnp.int32).reshape(N_GX, N_GY, 1)
    spared = (columns == chosen) & (layers[None, None, :] == N_GZ - 1)
    pressed = (columns == lowest) & (layers[None, None, :] == 0)
    jitter = jnp.where(spared, 0, jitter)
    jitter = jnp.where(pressed, SLOTS // 8, jitter)
    return (baseline[None, None, :] - jitter).astype(jnp.int32)


def draw_slot_cell(key, part):
    key = jax.random.fold_in(key, 12)
    offset_key, order_key, first_key, last_key = jax.random.split(key, 4)
    bricks = N_GX * N_GY * N_GZ
    stride = CX * CY * CZ // SLOTS
    offsets = jax.random.randint(offset_key, (bricks, SLOTS), 0, stride)
    first = jax.random.randint(first_key, (), 0, bricks)
    last = jax.random.randint(last_key, (), 0, bricks)
    offsets = offsets.at[first, 0].set(0).at[last, SLOTS - 1].set(stride - 1)
    slot_iota = jnp.arange(SLOTS, dtype=jnp.int32)[None, :]
    cells = slot_iota * stride + offsets
    scores = jax.random.randint(order_key, (bricks, SLOTS), 0, 1073741824 // SLOTS) * SLOTS + slot_iota
    order = jnp.argsort(scores, axis=1, stable=True).astype(jnp.int32)
    cells = jnp.take_along_axis(cells, order, axis=1)
    return cells.reshape(N_GX, N_GY, N_GZ * SLOTS).astype(jnp.int32)


def draw_shell_count(key, part):
    key = jax.random.fold_in(key, 13)
    count_key, place_key = jax.random.split(key)
    total = N_GX * N_GY * N_GZ * PART_DEV
    counts = jax.random.randint(count_key, (total,), SHELLS // 8, SHELLS + 1)
    place = jax.random.randint(place_key, (), 0, total)
    counts = counts.at[place].set(SHELLS).at[(place + 1) % total].set(SHELLS // 8)
    return counts.reshape(N_GX, N_GY, N_GZ * PART_DEV).astype(jnp.int32)


def draw_shell_inverse(key, part):
    key = jax.random.fold_in(key, 14)
    diag_key, off_key = jax.random.split(key)
    diagonal = jax.random.uniform(diag_key, (N_GX, N_GY, SHELLS, N_GZ * PART_DEV), jnp.float32, 0.6, 1.2)
    scattered = jax.random.uniform(off_key, (N_GX, N_GY, SHELLS, SHELLS, N_GZ * PART_DEV), jnp.float32, -1.0, 1.0) * (0.5 / SHELLS)
    identity = (jnp.arange(SHELLS)[:, None] == jnp.arange(SHELLS)[None, :])[None, None, :, :, None]
    return scattered + jnp.where(identity, diagonal[:, :, :, None, :], 0.0)


def place_ends(drawn, stream_key, smallest, high):
    shape = drawn.shape
    spot = [jax.random.randint(jax.random.fold_in(stream_key, axis), (), 0, shape[axis]) for axis in range(len(shape))]
    drawn = drawn.at[tuple(spot)].set(smallest)
    longest = shape.index(max(shape))
    spot[longest] = (spot[longest] + 1) % shape[longest]
    return drawn.at[tuple(spot)].set(high)


def block_levels(rng, extent, cuts, least, largest):
    gain = 1.0
    for axis_at, shards_of in cuts:
        draws = jax.random.uniform(jax.random.fold_in(jax.random.fold_in(rng, 6), axis_at), (shards_of,), jnp.float32, least / len(cuts), largest / len(cuts))
        gain = gain * jnp.repeat(jnp.exp(draws), extent[axis_at] // shards_of).reshape((-1,) + (1,) * (len(extent) - 1 - axis_at))
    return gain


def gaussian(rng, dims, scale, bound, shards=(), kind=jnp.bfloat16):
    factor_of = block_levels(rng, dims, shards, -0.22, 0.18) if shards else 1.0
    array = jax.random.normal(rng, dims, jnp.float32) * scale * factor_of
    return jnp.minimum(jnp.maximum(array, -bound), bound).astype(kind)


def setup_inputs(seed: int = 0) -> dict:
    splits = jax.random.split(jax.random.key(seed), 14)
    return {
        "electrolyte": gaussian(splits[0], (NX, NY, NZ), 1.0, 6.0, ((0, 4), (1, 8), (2, 8)), jnp.float32),
        "conductivity": jnp.clip(jnp.exp(math.log(3.0) - 2.3025851 * jax.random.uniform(splits[1], (NX, NY, NZ), jnp.float32) ** block_levels(splits[1], (NX, NY, NZ), ((0, 4), (1, 8), (2, 8)), -0.2, 0.2)), 0.3, 3.0),
        "phase_label": place_ends((jax.random.randint(splits[2], (NX, NY, NZ), 0, 2) < 1).astype(jnp.int32), jax.random.fold_in(splits[2], 1), 0, 1),
        "applied_current": jnp.clip(jax.random.uniform(splits[3], (1,), jnp.float32, 0.3, 1.0), 0.3, 1.0),
        "slot_count": draw_slot_count(jax.random.fold_in(splits[13], 71), 0),
        "slot_cell": draw_slot_cell(jax.random.fold_in(splits[13], 71), 0),
        "slot_label": place_ends(jax.random.randint(splits[6], (N_GX, N_GY, N_GZ * SLOTS), 0, COLUMN_PARTS), jax.random.fold_in(splits[6], 1), 0, COLUMN_PARTS - 1).astype(jnp.int32),
        "slot_area": jnp.clip(jnp.exp(math.log(2.0) - 1.3862944 * jax.random.uniform(splits[7], (N_GX, N_GY, N_GZ * SLOTS), jnp.float32) ** block_levels(splits[7], (N_GX, N_GY, N_GZ * SLOTS), ((0, 4), (1, 8), (2, 8)), -0.2, 0.2)), 0.5, 2.0),
        "slot_rate": jnp.clip(jnp.exp(math.log(3.0) - 2.3025851 * jax.random.uniform(splits[8], (N_GX, N_GY, N_GZ * SLOTS), jnp.float32) ** block_levels(splits[8], (N_GX, N_GY, N_GZ * SLOTS), ((0, 4), (1, 8), (2, 8)), -0.2, 0.2)), 0.3, 3.0),
        "owner_map": jax.vmap(lambda own: jax.random.permutation(own, COLUMN_PARTS))(jax.random.split(splits[9], N_GX * N_GY)).reshape((N_GX, N_GY, COLUMN_PARTS)).astype(jnp.int32),
        "shell_count": draw_shell_count(jax.random.fold_in(splits[13], 71), 0),
        "shell_conc": jnp.clip(0.2 + 0.7 * jax.random.uniform(splits[11], (N_GX, N_GY, SHELLS, COLUMN_PARTS), jnp.float32) ** block_levels(splits[11], (N_GX, N_GY, SHELLS, COLUMN_PARTS), ((0, 4), (1, 8), (3, 8)), -0.2, 0.2), 0.2, 0.9),
        "shell_inverse": draw_shell_inverse(jax.random.fold_in(splits[13], 71), 0),
    }


inv_step = 4.0
conc_coupling = 0.5
solid_factor = 0.1
shell_step = 0.02


def face_terms(padded):
    faces_x = 0.5 * (padded[:-1, 1:-1, 1:-1] + padded[1:, 1:-1, 1:-1])
    faces_y = 0.5 * (padded[1:-1, :-1, 1:-1] + padded[1:-1, 1:, 1:-1])
    faces_z = 0.5 * (padded[1:-1, 1:-1, :-1] + padded[1:-1, 1:-1, 1:])
    face_total = faces_x[:-1] + faces_x[1:] + faces_y[:, :-1] + faces_y[:, 1:] + faces_z[:, :, :-1] + faces_z[:, :, 1:]
    return faces_x, faces_y, faces_z, face_total


def neighbour_sum(padded, faces_x, faces_y, faces_z):
    result = faces_x[:-1] * padded[:, :-2, 1:-1, 1:-1] + faces_x[1:] * padded[:, 2:, 1:-1, 1:-1]
    result = result + faces_y[:, :-1] * padded[:, 1:-1, :-2, 1:-1] + faces_y[:, 1:] * padded[:, 1:-1, 2:, 1:-1]
    result = result + faces_z[:, :, :-1] * padded[:, 1:-1, 1:-1, :-2] + faces_z[:, :, 1:] * padded[:, 1:-1, 1:-1, 2:]
    return result


def relax_fields(padded, faces_x, faces_y, faces_z, system):
    beside_all = neighbour_sum(padded, faces_x, faces_y, faces_z)
    centre = padded[1, 1:-1, 1:-1, 1:-1]
    next_conc = (system[0] + beside_all[0] + system[4] * centre) * system[2]
    next_pot = (system[1] + beside_all[1]) * system[3]
    return jnp.stack([next_conc, next_pot])


def build_system(fields, padded, electrolyte, faces_x, faces_y, faces_z, face_total, source, uptake):
    laplace = neighbour_sum(padded, faces_x, faces_y, faces_z) - face_total * fields
    rhs_conc = laplace[0] - (fields[0] - electrolyte) * inv_step - conc_coupling * source
    rhs_pot = laplace[1] + source
    return jnp.stack([rhs_conc, rhs_pot, 1.0 / (inv_step + face_total), 1.0 / (face_total + uptake), conc_coupling * uptake])


def slot_terms(sampled, surface_conc, slot_area, slot_rate, solid_potential):
    open_circuit = 0.4 * jnp.tanh(3.0 * (0.5 - surface_conc))
    overpotential = solid_potential - sampled[1] - open_circuit
    growth = jnp.exp(0.5 * overpotential)
    factor = slot_rate * (1.0 + 0.5 * jnp.tanh(sampled[0]))
    flux_term = slot_area * factor * (growth - 1.0 / growth)
    slope_term = slot_area * factor * (0.5 * (growth + 1.0 / growth))
    return flux_term, slope_term


def to_bricks(grid):
    blocks = grid.reshape(N_GX, CX, N_GY, CY, N_GZ, CZ).transpose(0, 2, 4, 1, 3, 5)
    return blocks.reshape(N_GX, N_GY, N_GZ, CX * CY * CZ)


def from_bricks(blocks):
    grid = blocks.reshape(N_GX, N_GY, N_GZ, CX, CY, CZ).transpose(0, 3, 1, 4, 2, 5)
    return grid.reshape(N_GX * CX, N_GY * CY, N_GZ * CZ)


def reference(electrolyte, conductivity, phase_label, applied_current, slot_count, slot_cell, slot_label, slot_area, slot_rate, owner_map, shell_count, shell_conc, shell_inverse):
    brick_cells = CX * CY * CZ
    conductance = conductivity * jnp.where(phase_label == 1, solid_factor, 1.0)
    faces_x, faces_y, faces_z, face_total = face_terms(jnp.pad(conductance, 1))
    cell_index = slot_cell.reshape(N_GX, N_GY, N_GZ, SLOTS)
    area_four = slot_area.reshape(N_GX, N_GY, N_GZ, SLOTS)
    rate_four = slot_rate.reshape(N_GX, N_GY, N_GZ, SLOTS)
    live_mask = (jnp.arange(SLOTS, dtype=jnp.int32)[None, None, None, :] < slot_count[..., None]).astype(jnp.float32)
    position = jnp.take_along_axis(owner_map, slot_label, axis=2)
    shell_index = jnp.arange(SHELLS, dtype=jnp.int32)[:, None]
    surface_shell = shell_index[None, None] == (shell_count - 1)[:, :, None, :]
    surface_all = jnp.sum(jnp.where(surface_shell, shell_conc, 0.0), axis=2)
    surface_conc = jnp.take_along_axis(surface_all, position, axis=2).reshape(N_GX, N_GY, N_GZ, SLOTS)
    brick_ids = jnp.arange(N_GX * N_GY * N_GZ, dtype=jnp.int32).reshape(N_GX, N_GY, N_GZ, 1)
    flat_index = (brick_ids * brick_cells + cell_index).reshape(-1)

    def sample(fields):
        bricks = jnp.stack([to_bricks(fields[0]), to_bricks(fields[1])])
        return jnp.take_along_axis(bricks, cell_index[None], axis=4)

    def spread(values):
        flat = jnp.zeros((N_GX * N_GY * N_GZ * brick_cells,), jnp.float32).at[flat_index].add(values.reshape(-1))
        return from_bricks(flat.reshape(N_GX, N_GY, N_GZ, brick_cells))

    fields = jnp.stack([electrolyte, jnp.zeros_like(electrolyte)])
    solid_potential = jnp.zeros((), jnp.float32)
    margin = ((0, 0), (1, 1), (1, 1), (1, 1))
    for sweep_index in range(SWEEPS):
        sampled = sample(fields)
        flux_term, slope_term = slot_terms(sampled, surface_conc, area_four, rate_four, solid_potential)
        current_sum = jnp.sum(live_mask * flux_term)
        weight_sum = jnp.sum(live_mask * slope_term)
        area_sum = jnp.sum(live_mask * area_four)
        solid_potential = solid_potential + (applied_current[0] * area_sum - current_sum) / weight_sum
        flux_term, slope_term = slot_terms(sampled, surface_conc, area_four, rate_four, solid_potential)
        source = spread(live_mask * flux_term)
        uptake = spread(live_mask * slope_term)
        system = build_system(fields, jnp.pad(fields, margin), electrolyte, faces_x, faces_y, faces_z, face_total, source, uptake)
        correction = jnp.zeros_like(fields)
        for iteration in range(ITERS):
            correction = relax_fields(jnp.pad(correction, margin), faces_x, faces_y, faces_z, system)
        fields = fields + correction
    sampled = sample(fields)
    flux_term, slope_term = slot_terms(sampled, surface_conc, area_four, rate_four, solid_potential)
    column_ids = jnp.arange(N_GX * N_GY, dtype=jnp.int32).reshape(N_GX, N_GY, 1) * COLUMN_PARTS + position
    particle_flux = jax.ops.segment_sum((live_mask * flux_term).reshape(-1), column_ids.reshape(-1), num_segments=N_GX * N_GY * COLUMN_PARTS)
    particle_flux = particle_flux.reshape(N_GX, N_GY, COLUMN_PARTS)
    fill = (shell_index[None, None] < shell_count[:, :, None, :]).astype(jnp.float32)
    load = shell_conc * fill + shell_step * particle_flux[:, :, None, :] * surface_shell.astype(jnp.float32)
    updated = jnp.einsum("xyijq,xyjq->xyiq", shell_inverse, load, precision=lax.Precision.HIGHEST) * fill
    return fields[0], fields[1], updated
```

```python
import functools

import jax
import jax.numpy as jnp
from jax import lax
from jax.experimental import pallas as pl
from jax.experimental.pallas import tpu as pltpu
from jax.sharding import PartitionSpec as P

SWEEPS = 2
ITERS = 8

inv_step = 4.0
conc_coupling = 0.5
solid_factor = 0.1
shell_step = 0.02

ROWS = 160
FIRST = 16
TILES = 18
f32 = jnp.float32
bf16 = jnp.bfloat16
VMEM = pl.BlockSpec(memory_space=pltpu.VMEM)
SMEM = pl.BlockSpec(memory_space=pltpu.SMEM)


def params():
    return pltpu.CompilerParams(vmem_limit_bytes=56 * 1024 * 1024)


def iota(shape, dim):
    return lax.broadcasted_iota(jnp.int32, shape, dim)


def lookup(table_ref, rows, low, high, init):
    value = init
    for row in range(rows):
        line = jnp.broadcast_to(table_ref[pl.ds(row, 1), :], (8, 128))
        found = jnp.take_along_axis(line, low, axis=1)
        value = found if row == 0 else jnp.where(high == row, found, value)
    return value


def lookup_long(table_ref, rows, low, high):
    def step(row, values):
        line = jnp.broadcast_to(table_ref[pl.ds(row, 1), :], (8, 128))
        return tuple(
            jnp.where(high[8 * h : 8 * h + 8] == row, jnp.take_along_axis(line, low[8 * h : 8 * h + 8], axis=1), values[h])
            for h in range(2)
        )

    zero = jnp.zeros((8, 128), f32)
    return jnp.concatenate(lax.fori_loop(0, rows, step, (zero, zero), unroll=8), axis=0)


def split_value(value, pieces):
    out = []
    for _ in range(pieces):
        part = value.astype(bf16).astype(f32)
        out.append(part)
        value = value - part
    return out


def by_particle(value, position, left_ref, right_ref):
    parts = split_value(value, 3)
    low = jnp.bitwise_and(position, 127)
    high = jnp.right_shift(position, 7)
    row_high = iota((16, 128), 0)
    row_low = iota((128, 128), 0)
    for t in range(16):
        mask = row_high == high[t : t + 1]
        for n, part in enumerate(parts):
            left_ref[16 * n : 16 * n + 16, 128 * t : 128 * t + 128] = jnp.where(mask, part[t : t + 1], 0.0).astype(bf16)
        right_ref[:, 128 * t : 128 * t + 128] = jnp.where(row_low == low[t : t + 1], 1.0, 0.0).astype(bf16)
    total = lax.dot_general(left_ref[...], right_ref[...], (((1,), (1,)), ((), ())), preferred_element_type=f32)
    return total[0:8] + total[16:24] + total[32:40]


def open_circuit(surface_conc):
    return 0.4 * jnp.tanh(3.0 * (0.5 - surface_conc))


def prepare_kernel(
    conc_ref,
    cond_ref,
    phase_ref,
    count_ref,
    cell_ref,
    label_ref,
    area_ref,
    rate_ref,
    owner_ref,
    shells_ref,
    shell_conc_ref,
    fields_ref,
    z_low_ref,
    z_high_ref,
    column_ref,
    position_ref,
    flat_ref,
    owner_f_ref,
    high_ref,
    value_ref,
    left_ref,
    right_ref,
):
    lane = iota((16, 128), 1)
    slot = iota((16, 128), 0) * 128 + lane
    live = (slot < count_ref[0, 0, 0]).astype(f32)
    label = label_ref[...]
    owner_f_ref[...] = owner_ref[...].astype(f32)
    low = jnp.bitwise_and(label, 127)
    high = jnp.right_shift(label, 7)
    position = jnp.concatenate(
        [lookup(owner_f_ref, 8, low[h : h + 8], high[h : h + 8], None) for h in (0, 8)], axis=0
    ).astype(jnp.int32)
    position_ref[...] = position
    area = area_ref[...]
    weight = live * area * rate_ref[...]
    cell = cell_ref[...]
    cell_low = jnp.bitwise_and(cell, 127)
    cell_high = jnp.right_shift(cell, 7)

    parts = split_value(weight, 2) + [
        jnp.right_shift(position, 3).astype(f32),
        jnp.bitwise_and(position, 7).astype(f32),
    ]
    row_high = iota((256, 128), 0)
    row_low = iota((128, 128), 0)
    for t in range(16):
        columns = slice(128 * t, 128 * t + 128)
        high_ref[:, columns] = jnp.where(row_high == cell_high[t : t + 1], 1.0, 0.0).astype(bf16)
        mask = row_low == cell_low[t : t + 1]
        for n, part in enumerate(parts):
            value_ref[128 * n : 128 * n + 128, columns] = jnp.where(mask, part[t : t + 1], 0.0).astype(bf16)
    dense = lax.dot_general(high_ref[...], value_ref[...], (((1,), (1,)), ((), ())), preferred_element_type=f32)
    fields_ref[0] = conc_ref[...]
    fields_ref[1] = cond_ref[...] * jnp.where(phase_ref[...] == 1, solid_factor, 1.0)
    fields_ref[2] = (dense[:, 0:128] + dense[:, 128:256]).reshape(16, 16, 128)
    fields_ref[3] = (dense[:, 256:384] * 8.0 + dense[:, 384:512]).reshape(16, 16, 128)

    for f in range(4):
        z_low = jnp.zeros((16, 128), f32)
        z_high = jnp.zeros((16, 128), f32)
        for x in range(16):
            plane = fields_ref[f, x]
            mask = jnp.right_shift(lane, 3) == x
            z_low = jnp.where(mask, pltpu.roll(plane, 8 * x, 1) if x else plane, z_low)
            z_high = jnp.where(mask, pltpu.roll(plane, (8 * x + 8) % 128, 1) if x < 15 else plane, z_high)
        z_low_ref[f] = z_low
        z_high_ref[f] = z_high

    flat_ref[...] = conc_ref[...].reshape(256, 128)
    sampled = lookup_long(flat_ref, 256, cell_low, cell_high)
    summed = by_particle(weight * (1.0 + 0.5 * jnp.tanh(sampled)), position, left_ref, right_ref)
    surface_shell = iota((64, 128), 0) == shells_ref[...] - 1
    surface = jnp.sum(jnp.where(surface_shell, shell_conc_ref[...], 0.0), axis=0, keepdims=True)
    area_sum = jnp.sum(live * area, axis=0, keepdims=True)
    tail = jnp.concatenate([surface, area_sum, jnp.zeros((6, 128), f32)], axis=0)
    block = jnp.concatenate([summed, tail], axis=0)
    for n in range(8):
        column_ref[n] = block


def column_kernel(column_ref, sums_ref):
    weight = jnp.zeros((8, 128), f32)
    area = jnp.zeros((1, 128), f32)
    for n in range(8):
        weight = weight + column_ref[n, 0:8]
        area = area + column_ref[n, 9:10]
    surface = jnp.concatenate([column_ref[n, 8:9] for n in range(8)], axis=0)
    circuit = open_circuit(surface)
    growth = jnp.exp(-0.5 * circuit)
    shrink = jnp.exp(0.5 * circuit)
    current = jnp.sum(weight * (growth - shrink), axis=0, keepdims=True)
    slope = jnp.sum(weight * (0.5 * (growth + shrink)), axis=0, keepdims=True)
    block = jnp.concatenate([circuit, current, slope, area, jnp.zeros((5, 128), f32)], axis=0)
    for n in range(sums_ref.shape[0]):
        sums_ref[n] = block


def total_of(value):
    return jnp.sum(jnp.sum(value, axis=0, keepdims=True), axis=1, keepdims=True)


def shift(value, by):
    return pltpu.roll(value, by % 128, 1)


def widen(load, wide_ref):
    def square(planes):
        return jnp.concatenate([load(p, t) for p in planes for t in range(4)], axis=0).T

    for n in range(8):
        wide_ref[n, FIRST : FIRST + 128] = square((16 + n, n, 8 + n, 25 + n))
    ends = square((24, 34, 35, 33))
    for n in range(8):
        wide_ref[n, FIRST - 8 : FIRST] = ends[8 * n : 8 * n + 8]
        wide_ref[n, FIRST + 128 : FIRST + 136] = ends[64 + 8 * n : 72 + 8 * n]
        wide_ref[n, 0 : FIRST - 8] = jnp.zeros((8, 128), f32)
        wide_ref[n, FIRST + 136 : ROWS] = jnp.zeros((8, 128), f32)


def loader(f, centre_ref, ends_ref, x_low_ref, x_high_ref, y_low_ref, y_high_ref):
    def load(plane, tile):
        if tile == 0:
            return y_low_ref[f, plane]
        if tile == 3:
            return y_high_ref[f, plane]
        rows = slice(8 * tile - 8, 8 * tile)
        if plane < 16:
            return centre_ref[f, plane, rows]
        if plane < 25:
            return x_low_ref[f, plane - 16, rows]
        if plane < 34:
            return x_high_ref[f, plane - 25, rows]
        return ends_ref[f, plane - 34, rows]

    return load


def narrow(wide_ref, store):
    for n in range(8):
        square = wide_ref[n, FIRST : FIRST + 128].T
        store(n, square[40:56])
        store(8 + n, square[72:88])


def end_slabs(wide_ref):
    square = jnp.concatenate(
        [wide_ref[n, FIRST : FIRST + 8] for n in range(8)]
        + [wide_ref[n, FIRST + 120 : FIRST + 128] for n in range(8)],
        axis=0,
    ).T
    first, second = square[40:56], square[72:88]
    low_half = iota((16, 128), 1) < 64
    low = jnp.where(low_half, first, shift(second, 64))
    high = jnp.where(low_half, shift(first, 64), second)
    return low, high


def tiles(body, first=0, last=TILES):
    def step(n, carry):
        body(pl.multiple_of(8 + 8 * n, 8))
        return carry

    lax.fori_loop(first, last, step, 0)


def solve(c_ref, p_ref, start_ref, k_ref, w_ref, circuit_ref, solid, work):
    fx, fy, fz, rc, rp, gc, gp, coup, dc, dp = work

    def set_faces(r):
        k = [k_ref[n, pl.ds(r, 8)] for n in range(8)]
        for n in range(8):
            below = k[n - 1] if n else shift(k[7], 32)
            fx[n, pl.ds(r, 8)] = 0.5 * (k[n] + below)
            fy[n, pl.ds(r, 8)] = 0.5 * (k[n] + shift(k[n], 1))
            fz[n, pl.ds(r, 8)] = 0.5 * (k[n] + k_ref[n, pl.ds(r - 1, 8)])

    for n in range(8):
        fz[n, FIRST + 136 : ROWS] = jnp.zeros((8, 128), f32)
        for ref in (dc, dp):
            for b in range(2):
                ref[b, n, 0 : FIRST - 8] = jnp.zeros((8, 128), f32)
                ref[b, n, FIRST + 136 : ROWS] = jnp.zeros((8, 128), f32)
    tiles(set_faces)

    def faces(r):
        lower = [fx[n, pl.ds(r, 8)] for n in range(8)]
        return lower + [shift(lower[0], -32)]

    def beside(values, n, source, r, x_faces, y_face, z_face, z_next):
        low = values[n - 1] if n else shift(values[7], 32)
        high = values[n + 1] if n < 7 else shift(values[0], -32)
        total = x_faces[n] * low + x_faces[n + 1] * high
        total = total + (y_face * shift(values[n], 1) + shift(y_face * values[n], -1))
        return total + (z_face * source[n, pl.ds(r - 1, 8)] + z_next * source[n, pl.ds(r + 1, 8)])

    def set_system(r):
        rows = pl.ds(r, 8)
        c = [c_ref[n, rows] for n in range(8)]
        p = None if p_ref is None else [p_ref[n, rows] for n in range(8)]
        x_faces = faces(r)
        for n in range(8):
            y_face, z_face, z_next = fy[n, rows], fz[n, rows], fz[n, pl.ds(r + 1, 8)]
            face_total = x_faces[n] + x_faces[n + 1] + y_face + shift(y_face, -1) + z_face + z_next
            over = solid - circuit_ref[n, rows]
            if p is not None:
                over = over - p[n]
            growth = jnp.exp(0.5 * over)
            shrink = jnp.exp(-0.5 * over)
            factor = w_ref[n, rows] * (1.0 + 0.5 * jnp.tanh(c[n]))
            source = factor * (growth - shrink)
            uptake = factor * (0.5 * (growth + shrink))
            rhs_c = beside(c, n, c_ref, r, x_faces, y_face, z_face, z_next) - face_total * c[n] - conc_coupling * source
            rhs_p = source
            if p is not None:
                rhs_c = rhs_c - (c[n] - start_ref[n, rows]) * inv_step
                rhs_p = rhs_p + (beside(p, n, p_ref, r, x_faces, y_face, z_face, z_next) - face_total * p[n])
            inside = k_ref[n, rows] > 0.0
            recip_c = jnp.where(inside, 1.0 / (inv_step + face_total), 0.0)
            recip_p = jnp.where(inside, 1.0 / (face_total + uptake), 0.0)
            rc[n, rows] = rhs_c
            rp[n, rows] = rhs_p
            gc[n, rows] = recip_c
            gp[n, rows] = recip_p
            coup[n, rows] = conc_coupling * uptake
            dc[0, n, rows] = rhs_c * recip_c
            dp[0, n, rows] = rhs_p * recip_p

    tiles(set_system)

    def iteration(m, carry):
        now, then = m % 2, (m + 1) % 2
        c_now, p_now, c_then, p_then = dc.at[now], dp.at[now], dc.at[then], dp.at[then]

        def relax(r):
            rows = pl.ds(r, 8)
            c = [c_now[n, rows] for n in range(8)]
            p = [p_now[n, rows] for n in range(8)]
            x_faces = faces(r)
            for n in range(8):
                y_face, z_face, z_next = fy[n, rows], fz[n, rows], fz[n, pl.ds(r + 1, 8)]
                next_c = beside(c, n, c_now, r, x_faces, y_face, z_face, z_next)
                next_p = beside(p, n, p_now, r, x_faces, y_face, z_face, z_next)
                c_then[n, rows] = (rc[n, rows] + next_c + coup[n, rows] * p[n]) * gc[n, rows]
                p_then[n, rows] = (rp[n, rows] + next_p) * gp[n, rows]

        tiles(relax)
        return carry

    lax.fori_loop(0, ITERS - 1, iteration, 0)
    last = (ITERS - 1) % 2
    return dc.at[last], dp.at[last]


def first_kernel(
    coords_ref,
    current_ref,
    centre_ref,
    ends_ref,
    x_low_ref,
    x_high_ref,
    y_low_ref,
    y_high_ref,
    sums_ref,
    start_ref,
    k_ref,
    w_ref,
    circuit_ref,
    fields_ref,
    z_low_ref,
    z_high_ref,
    part_ref,
    state_ref,
    c_ref,
    table_ref,
    *work,
):
    pieces = (centre_ref, ends_ref, x_low_ref, x_high_ref, y_low_ref, y_high_ref)
    widen(loader(0, *pieces), start_ref)
    widen(loader(1, *pieces), k_ref)
    widen(loader(2, *pieces), w_ref)
    at_x, at_y, size_x, size_y = coords_ref[0], coords_ref[1], coords_ref[2], coords_ref[3]
    for i in range(3):
        for j in range(3):
            near_x = jnp.clip(at_x + (i - 1), 0, size_x - 1)
            near_y = jnp.clip(at_y + (j - 1), 0, size_y - 1)
            table_ref[3 * i + j] = sums_ref[near_x * size_y + near_y, 0:8]
    positions = loader(3, *pieces)

    def circuit(plane, tile):
        i = 0 if 16 <= plane < 25 else 2 if 25 <= plane < 34 else 1
        j = (0, 1, 1, 2)[tile]
        position = positions(plane, tile).astype(jnp.int32)
        return lookup(
            table_ref.at[3 * i + j], 8, jnp.bitwise_and(position, 127), jnp.right_shift(position, 7), None
        )

    widen(circuit, circuit_ref)

    sums = sums_ref[0, 8:16]
    for n in range(1, sums_ref.shape[0]):
        sums = sums + sums_ref[n, 8:16]
    sums = jnp.sum(sums, axis=1, keepdims=True)
    current, slope, area = sums[0:1], sums[1:2], sums[2:3]
    solid = (current_ref[0] * area - current) / slope
    dc, dp = solve(start_ref, None, start_ref, k_ref, w_ref, circuit_ref, solid, work)

    lane = iota((8, 128), 1)
    mine = (lane >= 32) & (lane < 96) & (lane % 32 >= 8) & (lane % 32 < 24)
    zero = jnp.zeros((8, 128), f32)

    def finish(n, carry):
        rows = pl.ds(pl.multiple_of(8 + 8 * n, 8), 8)
        total, weight = carry
        for m in range(8):
            c = start_ref[m, rows] + dc[m, rows]
            p = dp[m, rows]
            c_ref[m, rows] = c
            over = solid - p - circuit_ref[m, rows]
            growth = jnp.exp(0.5 * over)
            shrink = jnp.exp(-0.5 * over)
            factor = w_ref[m, rows] * (1.0 + 0.5 * jnp.tanh(c))
            total = total + factor * (growth - shrink)
            weight = weight + factor * (0.5 * (growth + shrink))
        return total, weight

    total, weight = lax.fori_loop(1, TILES - 1, finish, (zero, zero))
    total = total_of(jnp.where(mine, total, 0.0))
    weight = total_of(jnp.where(mine, weight, 0.0))
    row = iota((8, 128), 1)
    block = jnp.where(row == 0, total, jnp.where(row == 1, weight, 0.0))

    def spread(n, carry):
        part_ref[pl.ds(pl.multiple_of(8 * n, 8), 8)] = block
        return carry

    lax.fori_loop(0, part_ref.shape[0] // 8, spread, 0)
    state_ref[...] = jnp.where(row == 0, solid, jnp.where(row == 1, area, 0.0))
    for f, ref in enumerate((c_ref, dp)):

        def store(plane, value, f=f):
            fields_ref[f, plane] = value

        narrow(ref, store)
        z_low_ref[f], z_high_ref[f] = end_slabs(ref)


def second_kernel(
    current_ref,
    centre_ref,
    ends_ref,
    x_low_ref,
    x_high_ref,
    y_low_ref,
    y_high_ref,
    part_ref,
    state_ref,
    start_ref,
    k_ref,
    w_ref,
    circuit_ref,
    cell_ref,
    position_ref,
    conc_ref,
    pot_ref,
    flux_ref,
    c_ref,
    p_ref,
    flat_ref,
    left_ref,
    right_ref,
    *work,
):
    pieces = (centre_ref, ends_ref, x_low_ref, x_high_ref, y_low_ref, y_high_ref)
    widen(loader(0, *pieces), c_ref)
    widen(loader(1, *pieces), p_ref)
    sums = part_ref[0:8]
    for n in range(1, part_ref.shape[0] // 8):
        sums = sums + part_ref[8 * n : 8 * n + 8]
    sums = jnp.sum(sums, axis=0, keepdims=True)
    current, slope = sums[:, 0:1], sums[:, 1:2]
    before, area = state_ref[0:1, 0:1], state_ref[0:1, 1:2]
    solid = before + (current_ref[0] * area - current) / slope
    dc, dp = solve(c_ref, p_ref, start_ref, k_ref, w_ref, circuit_ref, solid, work)
    flux = work[0]

    def finish(r):
        rows = pl.ds(r, 8)
        for m in range(8):
            c = c_ref[m, rows] + dc[m, rows]
            p = p_ref[m, rows] + dp[m, rows]
            c_ref[m, rows] = c
            p_ref[m, rows] = p
            over = solid - p - circuit_ref[m, rows]
            factor = w_ref[m, rows] * (1.0 + 0.5 * jnp.tanh(c))
            flux[m, rows] = factor * (jnp.exp(0.5 * over) - jnp.exp(-0.5 * over))

    tiles(finish, 1, TILES - 1)

    def store_conc(plane, value):
        conc_ref[plane] = value

    def store_pot(plane, value):
        pot_ref[plane] = value

    def store_flux(plane, value):
        flat_ref[16 * plane : 16 * plane + 16] = value

    narrow(flux, store_flux)
    cell = cell_ref[...]
    sampled = lookup_long(flat_ref, 256, jnp.bitwise_and(cell, 127), jnp.right_shift(cell, 7))
    flux_ref[...] = by_particle(sampled, position_ref[...], left_ref, right_ref)
    narrow(c_ref, store_conc)
    narrow(p_ref, store_pot)


def shell_kernel(inverse_ref, shells_ref, conc_ref, base_ref, column_ref):
    count = shells_ref[...]
    index = iota((64, 128), 0)
    fill = (index < count).astype(f32)
    surface = index == count - 1
    load = conc_ref[...] * fill
    rows = inverse_ref.shape[0]
    base, column = [], []
    for i in range(rows):
        matrix = inverse_ref[i]
        base.append(jnp.sum(matrix * load, axis=0, keepdims=True))
        column.append(jnp.sum(jnp.where(surface, matrix, 0.0), axis=0, keepdims=True))
    keep = (iota((rows, 128), 0) + pl.program_id(0) * rows < count).astype(f32)
    base_ref[...] = jnp.concatenate(base, axis=0) * keep
    column_ref[...] = jnp.concatenate(column, axis=0) * keep


def swap(low, high, axis):
    count = lax.axis_size(axis)
    up = [(i, i + 1) for i in range(count - 1)]
    down = [(i + 1, i) for i in range(count - 1)]
    return lax.ppermute(high, axis, up), lax.ppermute(low, axis, down)


def exchange(fields, z_low, z_high):
    below, above = swap(z_low, z_high, "gz")
    first = jnp.concatenate([below[..., :64], above[..., :64]], axis=2)
    second = jnp.concatenate([below[..., 64:], above[..., 64:]], axis=2)
    ends = jnp.stack([first, second], axis=1)
    x_low, x_high = swap(
        jnp.concatenate([fields[:, :8], ends[:, :1]], axis=1),
        jnp.concatenate([fields[:, 8:], ends[:, 1:]], axis=1),
        "gx",
    )
    whole = [fields, x_low, x_high, ends]
    y_low, y_high = swap(
        jnp.concatenate([part[:, :, :8] for part in whole], axis=1),
        jnp.concatenate([part[:, :, 8:] for part in whole], axis=1),
        "gy",
    )
    return fields, ends, x_low, x_high, y_low, y_high


def shape(*dims, dtype=f32):
    return jax.ShapeDtypeStruct(dims, dtype)


def wide_scratch(count):
    return [pltpu.VMEM((8, ROWS, 128), f32) for _ in range(count)]


def work_scratch():
    return wide_scratch(8) + [pltpu.VMEM((2, 8, ROWS, 128), f32) for _ in range(2)]


def on_device(
    electrolyte,
    conductivity,
    phase_label,
    applied_current,
    slot_count,
    slot_cell,
    slot_label,
    slot_area,
    slot_rate,
    owner_map,
    shell_count,
    shell_conc,
    shell_inverse,
):
    size_x, size_y, size_z = (lax.axis_size(a) for a in ("gx", "gy", "gz"))
    cell = slot_cell.reshape(16, 128)
    shells = shell_count.reshape(1, 128)
    conc = shell_conc.reshape(64, 128)
    fields, z_low, z_high, column, position = pl.pallas_call(
        prepare_kernel,
        in_specs=[VMEM] * 3 + [SMEM] + [VMEM] * 7,
        out_specs=[VMEM] * 5,
        out_shape=[
            shape(4, 16, 16, 128),
            shape(4, 16, 128),
            shape(4, 16, 128),
            shape(8, 16, 128),
            shape(16, 128, dtype=jnp.int32),
        ],
        scratch_shapes=[
            pltpu.VMEM((256, 128), f32),
            pltpu.VMEM((8, 128), f32),
            pltpu.VMEM((256, 2048), bf16),
            pltpu.VMEM((512, 2048), bf16),
            pltpu.VMEM((48, 2048), bf16),
            pltpu.VMEM((128, 2048), bf16),
        ],
        compiler_params=params(),
        name="prepare",
    )(
        electrolyte,
        conductivity,
        phase_label,
        slot_count,
        cell,
        slot_label.reshape(16, 128),
        slot_area.reshape(16, 128),
        slot_rate.reshape(16, 128),
        owner_map.reshape(8, 128),
        shells,
        conc,
    )
    pieces = exchange(fields, z_low, z_high)
    column = lax.all_to_all(column, "gz", 0, 0, tiled=True)
    sums = pl.pallas_call(
        column_kernel,
        in_specs=[VMEM],
        out_specs=VMEM,
        out_shape=shape(size_x * size_y, 16, 128),
        compiler_params=params(),
        name="column",
    )(column)
    sums = lax.all_to_all(sums, ("gx", "gy"), 0, 0, tiled=True)
    coords = jnp.stack([lax.axis_index("gx"), lax.axis_index("gy"), jnp.int32(size_x), jnp.int32(size_y)]).astype(jnp.int32)
    wide = shape(8, ROWS, 128)
    devices = size_x * size_y * size_z
    start, k, w, circuit, fields, z_low, z_high, part, state = pl.pallas_call(
        first_kernel,
        in_specs=[SMEM] * 2 + [VMEM] * 7,
        out_specs=[VMEM] * 9,
        out_shape=[
            wide,
            wide,
            wide,
            wide,
            shape(2, 16, 16, 128),
            shape(2, 16, 128),
            shape(2, 16, 128),
            shape(devices, 128),
            shape(8, 128),
        ],
        scratch_shapes=wide_scratch(1) + [pltpu.VMEM((9, 8, 128), f32)] + work_scratch(),
        compiler_params=params(),
        name="first_sweep",
    )(coords, applied_current, *pieces, sums)
    pieces = exchange(fields, z_low, z_high)
    part = lax.all_to_all(part, ("gx", "gy", "gz"), 0, 0, tiled=True)
    concentration, potential, flux = pl.pallas_call(
        second_kernel,
        in_specs=[SMEM] + [VMEM] * 14,
        out_specs=[VMEM] * 3,
        out_shape=[shape(16, 16, 128), shape(16, 16, 128), shape(8, 128)],
        scratch_shapes=wide_scratch(2)
        + [pltpu.VMEM((256, 128), f32), pltpu.VMEM((48, 2048), bf16), pltpu.VMEM((128, 2048), bf16)]
        + work_scratch(),
        compiler_params=params(),
        name="second_sweep",
    )(applied_current, *pieces, part, state, start, k, w, circuit, cell, position)
    base, surface_column = pl.pallas_call(
        shell_kernel,
        grid=(8,),
        in_specs=[
            pl.BlockSpec((8, 64, 128), lambda i: (i, 0, 0)),
            pl.BlockSpec((1, 128), lambda i: (0, 0)),
            pl.BlockSpec((64, 128), lambda i: (0, 0)),
        ],
        out_specs=[pl.BlockSpec((8, 128), lambda i: (i, 0))] * 2,
        out_shape=[shape(64, 128)] * 2,
        compiler_params=params(),
        name="shells",
    )(shell_inverse.reshape(64, 64, 128), shells, conc)
    flux = jnp.sum(lax.all_to_all(flux, "gz", 0, 0, tiled=True), axis=0, keepdims=True)
    updated = base + shell_step * flux * surface_column
    return (concentration, potential, updated[None, None])


def solution(mesh):
    placed = (
        P("gx", "gy", "gz"),
        P("gx", "gy", "gz"),
        P("gx", "gy", "gz"),
        P(),
        P("gx", "gy", "gz"),
        P("gx", "gy", "gz"),
        P("gx", "gy", "gz"),
        P("gx", "gy", "gz"),
        P("gx", "gy", "gz"),
        P("gx", "gy", None),
        P("gx", "gy", "gz"),
        P("gx", "gy", None, "gz"),
        P("gx", "gy", None, None, "gz"),
    )
    return jax.shard_map(
        on_device,
        mesh=mesh,
        in_specs=placed,
        out_specs=(P("gx", "gy", "gz"), P("gx", "gy", "gz"), P("gx", "gy", None, "gz")),
        check_vma=False,
    )
```

```python
import functools

import jax
import jax.numpy as jnp
from jax import lax
from jax.experimental import pallas as pl
from jax.experimental.pallas import tpu as pltpu
from jax.sharding import PartitionSpec as P

SWEEPS = 2
ITERS = 8

inv_step = 4.0
conc_coupling = 0.5
solid_factor = 0.1
shell_step = 0.02

ROWS = 160
FIRST = 16
TILES = 18
UNROLL = 18
PART_ROWS = 2
SUM_ROWS = 40
SETUP = 6
LAST = 4
f32 = jnp.float32
bf16 = jnp.bfloat16
VMEM = pl.BlockSpec(memory_space=pltpu.VMEM)
SMEM = pl.BlockSpec(memory_space=pltpu.SMEM)
HBM = pl.BlockSpec(memory_space=pltpu.HBM)


LONG = pl.CostEstimate(flops=0, bytes_accessed=160 * 1024 * 1024, transcendentals=0)


def params(mebibytes=24):
    return pltpu.CompilerParams(vmem_limit_bytes=mebibytes * 1024 * 1024)


def in_hbm(*arrays):
    return [pltpu.with_memory_space_constraint(array, pltpu.HBM) for array in arrays]


def copies(sources, targets, sems):
    return [pltpu.make_async_copy(s, t, sems.at[n]) for n, (s, t) in enumerate(zip(sources, targets))]


def iota(shape, dim):
    return lax.broadcasted_iota(jnp.int32, shape, dim)


def lookup(table_ref, rows, low, high, init):
    value = init
    for row in range(rows):
        line = jnp.broadcast_to(table_ref[pl.ds(row, 1), :], (8, 128))
        found = jnp.take_along_axis(line, low, axis=1)
        value = found if row == 0 else jnp.where(high == row, found, value)
    return value


def split_value(value, pieces):
    out = []
    for _ in range(pieces):
        part = value.astype(bf16).astype(f32)
        out.append(part)
        value = value - part
    return out


def by_particle(value, position, left_ref, right_ref):
    parts = split_value(value, 3)
    low = jnp.bitwise_and(position, 127)
    high = jnp.right_shift(position, 7)
    row_high = iota((16, 128), 0)
    row_low = iota((128, 128), 0)
    for t in range(16):
        mask = row_high == high[t : t + 1]
        for n, part in enumerate(parts):
            left_ref[16 * n : 16 * n + 16, 128 * t : 128 * t + 128] = jnp.where(mask, part[t : t + 1], 0.0).astype(bf16)
        right_ref[:, 128 * t : 128 * t + 128] = jnp.where(row_low == low[t : t + 1], 1.0, 0.0).astype(bf16)
    total = lax.dot_general(left_ref[...], right_ref[...], (((1,), (1,)), ((), ())), preferred_element_type=f32)
    return total[0:8] + total[16:24] + total[32:40]


def mark_rows(cell, high_ref):
    high = jnp.right_shift(cell, 7)
    row = iota((256, 128), 0)
    for t in range(16):
        high_ref[:, 128 * t : 128 * t + 128] = jnp.where(row == high[t : t + 1], 1.0, 0.0).astype(bf16)


def sample(flat, cell, high_ref):
    parts = split_value(flat.T, 2)
    left = jnp.concatenate(parts, axis=0).astype(bf16)
    low = jnp.bitwise_and(cell, 127)
    row = iota((128, 128), 0)
    out = []
    for t in range(0, 16, 2):
        found = jnp.dot(left, high_ref[:, 128 * t : 128 * t + 256], preferred_element_type=f32)
        found = found[0:128] + found[128:256]
        for u in range(2):
            mask = row == low[t + u : t + u + 1]
            out.append(jnp.sum(jnp.where(mask, found[:, 128 * u : 128 * u + 128], 0.0), axis=0, keepdims=True))
    return jnp.concatenate(out, axis=0)


def open_circuit(surface_conc):
    return 0.4 * jnp.tanh(3.0 * (0.5 - surface_conc))


def prepare_kernel(
    place_ref,
    count_ref,
    cell_hbm,
    label_hbm,
    owner_hbm,
    area_hbm,
    rate_hbm,
    conc_hbm,
    cond_hbm,
    phase_hbm,
    shells_hbm,
    shell_conc_hbm,
    fields_ref,
    z_first_ref,
    z_second_ref,
    column_ref,
    position_ref,
    owner_f_ref,
    high_ref,
    value_ref,
    left_ref,
    right_ref,
    cell_ref,
    label_ref,
    owner_ref,
    area_ref,
    rate_ref,
    conc_ref,
    cond_ref,
    phase_ref,
    shells_ref,
    shell_conc_ref,
    sems,
):
    held = (cell_ref, label_ref, owner_ref, area_ref, rate_ref, conc_ref, cond_ref, phase_ref, shells_ref, shell_conc_ref)
    given = (cell_hbm, label_hbm, owner_hbm, area_hbm, rate_hbm, conc_hbm, cond_hbm, phase_hbm, shells_hbm, shell_conc_hbm)
    reads = copies(given, held, sems)
    for read in reads:
        read.start()
    for read in reads:
        read.wait()
    lane = iota((16, 128), 1)
    slot = iota((16, 128), 0) * 128 + lane
    live = (slot < count_ref[0, 0, 0]).astype(f32)
    label = label_ref[...]
    owner_f_ref[...] = owner_ref[...].astype(f32)
    low = jnp.bitwise_and(label, 127)
    high = jnp.right_shift(label, 7)
    position = jnp.concatenate(
        [lookup(owner_f_ref, 8, low[h : h + 8], high[h : h + 8], None) for h in (0, 8)], axis=0
    ).astype(jnp.int32)
    position_ref[...] = position
    area = area_ref[...]
    weight = live * area * rate_ref[...]
    cell = cell_ref[...]
    cell_low = jnp.bitwise_and(cell, 127)
    mark_rows(cell, high_ref)

    parts = split_value(weight, 2) + [
        jnp.right_shift(position, 3).astype(f32),
        jnp.bitwise_and(position, 7).astype(f32),
    ]
    row_low = iota((128, 128), 0)
    for t in range(16):
        columns = slice(128 * t, 128 * t + 128)
        mask = row_low == cell_low[t : t + 1]
        for n, part in enumerate(parts):
            value_ref[128 * n : 128 * n + 128, columns] = jnp.where(mask, part[t : t + 1], 0.0).astype(bf16)
    dense = lax.dot_general(high_ref[...], value_ref[...], (((1,), (1,)), ((), ())), preferred_element_type=f32)
    fields_ref[0] = conc_ref[...]
    fields_ref[1] = cond_ref[...] * jnp.where(phase_ref[...] == 1, solid_factor, 1.0)
    fields_ref[2] = (dense[:, 0:128] + dense[:, 128:256]).reshape(16, 16, 128)
    fields_ref[3] = (dense[:, 256:384] * 8.0 + dense[:, 384:512]).reshape(16, 16, 128)

    for f in range(4):
        z_low = jnp.zeros((16, 128), f32)
        z_high = jnp.zeros((16, 128), f32)
        for x in range(16):
            plane = fields_ref[f, x]
            mask = jnp.right_shift(lane, 3) == x
            z_low = jnp.where(mask, pltpu.roll(plane, 8 * x, 1) if x else plane, z_low)
            z_high = jnp.where(mask, pltpu.roll(plane, (8 * x + 8) % 128, 1) if x < 15 else plane, z_high)
        z_first_ref[f], z_second_ref[f] = give(place_ref[6] == 0, z_low, z_high)

    sampled = sample(conc_ref[...].reshape(256, 128), cell, high_ref)
    summed = by_particle(weight * (1.0 + 0.5 * jnp.tanh(sampled)), position, left_ref, right_ref)
    surface_shell = iota((64, 128), 0) == shells_ref[...] - 1
    surface = jnp.sum(jnp.where(surface_shell, shell_conc_ref[...], 0.0), axis=0, keepdims=True)
    area_sum = jnp.sum(live * area, axis=0, keepdims=True)
    tail = jnp.concatenate([surface, area_sum, jnp.zeros((6, 128), f32)], axis=0)
    block = jnp.concatenate([summed, tail], axis=0)
    for n in range(8):
        column_ref[n] = block


def column_kernel(column_ref, sums_ref):
    weight = jnp.zeros((8, 128), f32)
    area = jnp.zeros((1, 128), f32)
    for n in range(8):
        weight = weight + column_ref[n, 0:8]
        area = area + column_ref[n, 9:10]
    surface = jnp.concatenate([column_ref[n, 8:9] for n in range(8)], axis=0)
    circuit = open_circuit(surface)
    growth = jnp.exp(-0.5 * circuit)
    shrink = jnp.exp(0.5 * circuit)
    current = jnp.sum(weight * (growth - shrink), axis=0, keepdims=True)
    slope = jnp.sum(weight * (0.5 * (growth + shrink)), axis=0, keepdims=True)
    block = jnp.concatenate([circuit, current, slope, area, jnp.zeros((5, 128), f32)], axis=0)
    for n in range(sums_ref.shape[0]):
        sums_ref[n, 0:16] = block
        sums_ref[n, 16:SUM_ROWS] = jnp.zeros((SUM_ROWS - 16, 128), f32)


def total_of(value):
    return jnp.sum(jnp.sum(value, axis=0, keepdims=True), axis=1, keepdims=True)


def shift(value, by):
    return pltpu.roll(value, by % 128, 1)


def widen(load, wide_ref):
    def square(planes):
        return jnp.concatenate([load(p, t) for p in planes for t in range(4)], axis=0).T

    for n in range(8):
        wide_ref[n, FIRST : FIRST + 128] = square((16 + n, n, 8 + n, 25 + n))
    ends = square((24, 34, 35, 33))
    for n in range(8):
        wide_ref[n, FIRST - 8 : FIRST] = ends[8 * n : 8 * n + 8]
        wide_ref[n, FIRST + 128 : FIRST + 136] = ends[64 + 8 * n : 72 + 8 * n]
        wide_ref[n, 0 : FIRST - 8] = jnp.zeros((8, 128), f32)
        wide_ref[n, FIRST + 136 : ROWS] = jnp.zeros((8, 128), f32)


def loader(f, place_ref, centre_ref, ends_ref, x_first_ref, x_second_ref, y_first_ref, y_second_ref):
    even_x, even_y = place_ref[4] == 0, place_ref[5] == 0

    def load(plane, tile):
        if tile in (0, 3):
            return take(even_y, y_first_ref[f, plane], y_second_ref[f, plane])[tile // 3]
        rows = slice(8 * tile - 8, 8 * tile)
        if plane < 16:
            return centre_ref[f, plane, rows]
        if plane < 34:
            side, n = divmod(plane - 16, 9)
            return take(even_x, x_first_ref[f, n, rows], x_second_ref[f, n, rows])[side]
        return ends_ref[f, plane - 34, rows]

    return load


def narrow(wide_ref, store):
    for n in range(8):
        square = wide_ref[n, FIRST : FIRST + 128].T
        store(n, square[40:56])
        store(8 + n, square[72:88])


def end_slabs(wide_ref):
    square = jnp.concatenate(
        [wide_ref[n, FIRST : FIRST + 8] for n in range(8)]
        + [wide_ref[n, FIRST + 120 : FIRST + 128] for n in range(8)],
        axis=0,
    ).T
    first, second = square[40:56], square[72:88]
    low_half = iota((16, 128), 1) < 64
    low = jnp.where(low_half, first, shift(second, 64))
    high = jnp.where(low_half, shift(first, 64), second)
    return low, high


def tiles(body, first=0, last=TILES, unroll=1):
    def step(n, carry):
        body(pl.multiple_of(8 + 8 * n, 8))
        return carry

    lax.fori_loop(first, last, step, 0, unroll=unroll)


def solve(c_ref, p_ref, start_ref, k_ref, w_ref, circuit_ref, solid, work):
    fx, fy, fz, rc, rp, gc, gp, coup, dc, dp, dc_next, dp_next = work

    def set_faces(r):
        k = [k_ref[n, pl.ds(r, 8)] for n in range(8)]
        for n in range(8):
            below = k[n - 1] if n else shift(k[7], 32)
            fx[n, pl.ds(r, 8)] = 0.5 * (k[n] + below)
            fy[n, pl.ds(r, 8)] = 0.5 * (k[n] + shift(k[n], 1))
            fz[n, pl.ds(r, 8)] = 0.5 * (k[n] + k_ref[n, pl.ds(r - 1, 8)])

    for n in range(8):
        fz[n, FIRST + 136 : ROWS] = jnp.zeros((8, 128), f32)
        for ref in (dc, dp, dc_next, dp_next):
            ref[n, 0 : FIRST - 8] = jnp.zeros((8, 128), f32)
            ref[n, FIRST + 136 : ROWS] = jnp.zeros((8, 128), f32)
    tiles(set_faces, unroll=SETUP)

    def faces(r):
        lower = [fx[n, pl.ds(r, 8)] for n in range(8)]
        return lower + [shift(lower[0], -32)]

    def beside(values, n, source, r, x_faces, y_face, z_face, z_next):
        low = values[n - 1] if n else shift(values[7], 32)
        high = values[n + 1] if n < 7 else shift(values[0], -32)
        total = x_faces[n] * low + x_faces[n + 1] * high
        total = total + (y_face * shift(values[n], 1) + shift(y_face * values[n], -1))
        return total + (z_face * source[n, pl.ds(r - 1, 8)] + z_next * source[n, pl.ds(r + 1, 8)])

    def set_system(r):
        rows = pl.ds(r, 8)
        c = [c_ref[n, rows] for n in range(8)]
        p = None if p_ref is None else [p_ref[n, rows] for n in range(8)]
        x_faces = faces(r)
        for n in range(8):
            y_face, z_face, z_next = fy[n, rows], fz[n, rows], fz[n, pl.ds(r + 1, 8)]
            face_total = x_faces[n] + x_faces[n + 1] + y_face + shift(y_face, -1) + z_face + z_next
            over = solid - circuit_ref[n, rows]
            if p is not None:
                over = over - p[n]
            growth = jnp.exp(0.5 * over)
            shrink = jnp.exp(-0.5 * over)
            factor = w_ref[n, rows] * (1.0 + 0.5 * jnp.tanh(c[n]))
            source = factor * (growth - shrink)
            uptake = factor * (0.5 * (growth + shrink))
            rhs_c = beside(c, n, c_ref, r, x_faces, y_face, z_face, z_next) - face_total * c[n] - conc_coupling * source
            rhs_p = source
            if p is not None:
                rhs_c = rhs_c - (c[n] - start_ref[n, rows]) * inv_step
                rhs_p = rhs_p + (beside(p, n, p_ref, r, x_faces, y_face, z_face, z_next) - face_total * p[n])
            inside = k_ref[n, rows] > 0.0
            recip_c = jnp.where(inside, 1.0 / (inv_step + face_total), 0.0)
            recip_p = jnp.where(inside, 1.0 / (face_total + uptake), 0.0)
            rc[n, rows] = rhs_c
            rp[n, rows] = rhs_p
            gc[n, rows] = recip_c
            gp[n, rows] = recip_p
            coup[n, rows] = conc_coupling * uptake
            dc[n, rows] = rhs_c * recip_c
            dp[n, rows] = rhs_p * recip_p

    tiles(set_system, unroll=SETUP)

    def iteration(c_now, p_now, c_then, p_then):
        def relax(r):
            rows = pl.ds(r, 8)
            c = [c_now[n, rows] for n in range(8)]
            p = [p_now[n, rows] for n in range(8)]
            x_faces = faces(r)
            for n in range(8):
                y_face, z_face, z_next = fy[n, rows], fz[n, rows], fz[n, pl.ds(r + 1, 8)]
                next_c = beside(c, n, c_now, r, x_faces, y_face, z_face, z_next)
                next_p = beside(p, n, p_now, r, x_faces, y_face, z_face, z_next)
                c_then[n, rows] = (rc[n, rows] + next_c + coup[n, rows] * p[n]) * gc[n, rows]
                p_then[n, rows] = (rp[n, rows] + next_p) * gp[n, rows]

        tiles(relax, unroll=UNROLL)

    def pair(_, carry):
        iteration(dc, dp, dc_next, dp_next)
        iteration(dc_next, dp_next, dc, dp)
        return carry

    lax.fori_loop(0, (ITERS - 1) // 2, pair, 0)
    if ITERS % 2 == 0:
        iteration(dc, dp, dc_next, dp_next)
        return dc_next, dp_next
    return dc, dp


def first_kernel(
    place_ref,
    current_ref,
    centre_ref,
    ends_ref,
    x_first_ref,
    x_second_ref,
    y_first_ref,
    y_second_ref,
    sums_ref,
    start_hbm,
    k_hbm,
    w_hbm,
    circuit_hbm,
    fields_ref,
    z_first_ref,
    z_second_ref,
    part_ref,
    state_ref,
    start_ref,
    k_ref,
    w_ref,
    circuit_ref,
    sems,
    c_ref,
    table_ref,
    *work,
):
    writes = copies((start_ref, k_ref, w_ref, circuit_ref), (start_hbm, k_hbm, w_hbm, circuit_hbm), sems)
    pieces = (place_ref, centre_ref, ends_ref, x_first_ref, x_second_ref, y_first_ref, y_second_ref)
    widen(loader(0, *pieces), start_ref)
    widen(loader(1, *pieces), k_ref)
    widen(loader(2, *pieces), w_ref)
    at_x, at_y, size_x, size_y = place_ref[0], place_ref[1], place_ref[2], place_ref[3]
    for i in range(3):
        for j in range(3):
            near_x = jnp.clip(at_x + (i - 1), 0, size_x - 1)
            near_y = jnp.clip(at_y + (j - 1), 0, size_y - 1)
            table_ref[3 * i + j] = sums_ref[near_x * size_y + near_y, 0:8]
    positions = loader(3, *pieces)

    def circuit(plane, tile):
        i = 0 if 16 <= plane < 25 else 2 if 25 <= plane < 34 else 1
        j = (0, 1, 1, 2)[tile]
        position = positions(plane, tile).astype(jnp.int32)
        return lookup(
            table_ref.at[3 * i + j], 8, jnp.bitwise_and(position, 127), jnp.right_shift(position, 7), None
        )

    widen(circuit, circuit_ref)
    for write in writes:
        write.start()

    sums = sums_ref[0, 8:16]
    for n in range(1, sums_ref.shape[0]):
        sums = sums + sums_ref[n, 8:16]
    sums = jnp.sum(sums, axis=1, keepdims=True)
    current, slope, area = sums[0:1], sums[1:2], sums[2:3]
    solid = (current_ref[0] * area - current) / slope
    dc, dp = solve(start_ref, None, start_ref, k_ref, w_ref, circuit_ref, solid, work)

    lane = iota((8, 128), 1)
    mine = (lane >= 32) & (lane < 96) & (lane % 32 >= 8) & (lane % 32 < 24)
    zero = jnp.zeros((8, 128), f32)

    def finish(n, carry):
        rows = pl.ds(pl.multiple_of(8 + 8 * n, 8), 8)
        total, weight = carry
        for m in range(8):
            c = start_ref[m, rows] + dc[m, rows]
            p = dp[m, rows]
            c_ref[m, rows] = c
            over = solid - p - circuit_ref[m, rows]
            growth = jnp.exp(0.5 * over)
            shrink = jnp.exp(-0.5 * over)
            factor = w_ref[m, rows] * (1.0 + 0.5 * jnp.tanh(c))
            total = total + factor * (growth - shrink)
            weight = weight + factor * (0.5 * (growth + shrink))
        return total, weight

    total, weight = lax.fori_loop(1, TILES - 1, finish, (zero, zero), unroll=LAST)
    total = total_of(jnp.where(mine, total, 0.0))
    weight = total_of(jnp.where(mine, weight, 0.0))
    row = iota((8, 128), 1)
    block = jnp.where(row == 0, total, jnp.where(row == 1, weight, 0.0))

    def spread(n, carry):
        part_ref[n] = block[: part_ref.shape[1]]
        return carry

    lax.fori_loop(0, part_ref.shape[0], spread, 0, unroll=8)
    state_ref[...] = jnp.where(row == 0, solid, jnp.where(row == 1, area, 0.0))
    for f, ref in enumerate((c_ref, dp)):

        def store(plane, value, f=f):
            fields_ref[f, plane] = value

        narrow(ref, store)
        z_first_ref[f], z_second_ref[f] = give(place_ref[6] == 0, *end_slabs(ref))
    for write in writes:
        write.wait()


def second_kernel(
    place_ref,
    current_ref,
    centre_ref,
    ends_ref,
    x_first_ref,
    x_second_ref,
    y_first_ref,
    y_second_ref,
    part_ref,
    state_ref,
    cell_ref,
    position_ref,
    start_hbm,
    k_hbm,
    w_hbm,
    circuit_hbm,
    conc_ref,
    pot_ref,
    flux_ref,
    start_ref,
    k_ref,
    w_ref,
    circuit_ref,
    sems,
    c_ref,
    p_ref,
    flat_ref,
    high_ref,
    left_ref,
    right_ref,
    *work,
):
    pieces = (place_ref, centre_ref, ends_ref, x_first_ref, x_second_ref, y_first_ref, y_second_ref)
    reads = copies((start_hbm, k_hbm, w_hbm, circuit_hbm), (start_ref, k_ref, w_ref, circuit_ref), sems)
    for read in reads:
        read.start()
    widen(loader(0, *pieces), c_ref)
    widen(loader(1, *pieces), p_ref)
    for read in reads:
        read.wait()
    sums = part_ref[0]
    for n in range(1, part_ref.shape[0]):
        sums = sums + part_ref[n]
    sums = sums[0:1]
    current, slope = sums[:, 0:1], sums[:, 1:2]
    before, area = state_ref[0:1, 0:1], state_ref[0:1, 1:2]
    solid = before + (current_ref[0] * area - current) / slope
    dc, dp = solve(c_ref, p_ref, start_ref, k_ref, w_ref, circuit_ref, solid, work)
    flux = work[0]

    def finish(r):
        rows = pl.ds(r, 8)
        for m in range(8):
            c = c_ref[m, rows] + dc[m, rows]
            p = p_ref[m, rows] + dp[m, rows]
            c_ref[m, rows] = c
            p_ref[m, rows] = p
            over = solid - p - circuit_ref[m, rows]
            factor = w_ref[m, rows] * (1.0 + 0.5 * jnp.tanh(c))
            flux[m, rows] = factor * (jnp.exp(0.5 * over) - jnp.exp(-0.5 * over))

    tiles(finish, 1, TILES - 1, unroll=LAST)

    def store_conc(plane, value):
        conc_ref[plane] = value

    def store_pot(plane, value):
        pot_ref[plane] = value

    def store_flux(plane, value):
        flat_ref[16 * plane : 16 * plane + 16] = value

    narrow(flux, store_flux)
    cell = cell_ref[...]
    mark_rows(cell, high_ref)
    sampled = sample(flat_ref[...], cell, high_ref)
    flux_ref[...] = by_particle(sampled, position_ref[...], left_ref, right_ref)
    narrow(c_ref, store_conc)
    narrow(p_ref, store_pot)


def shell_kernel(inverse_ref, shells_ref, conc_ref, base_ref, column_ref):
    count = shells_ref[...]
    index = iota((64, 128), 0)
    fill = (index < count).astype(f32)
    surface = index == count - 1
    load = conc_ref[...] * fill
    rows = inverse_ref.shape[0]
    base, column = [], []
    for i in range(rows):
        matrix = inverse_ref[i]
        base.append(jnp.sum(matrix * load, axis=0, keepdims=True))
        column.append(jnp.sum(jnp.where(surface, matrix, 0.0), axis=0, keepdims=True))
    keep = (iota((rows, 128), 0) + pl.program_id(0) * rows < count).astype(f32)
    base_ref[...] = jnp.concatenate(base, axis=0) * keep
    column_ref[...] = jnp.concatenate(column, axis=0) * keep


def trade(first, second, axis):
    count = lax.axis_size(axis)
    pairs = [(i, i ^ 1) for i in range(count)]
    others = [(i, i + 1) for i in range(1, count - 1, 2)]
    others = others + [(target, source) for source, target in others]
    return lax.ppermute(first, axis, pairs), lax.ppermute(second, axis, others)


def give(even, low, high):
    return jnp.where(even, high, low), jnp.where(even, low, high)


def take(even, first, second):
    return jnp.where(even, second, first), jnp.where(even, first, second)


def pack_x_kernel(place_ref, fields_ref, z_first_ref, z_second_ref, *rest):
    x_first_ref, x_second_ref, ends_ref = rest[-3:]
    even_x, even_z = place_ref[4] == 0, place_ref[6] == 0
    low_half = iota((16, 128), 1) < 64
    for f in range(fields_ref.shape[0]):
        below, above = take(even_z, z_first_ref[f], z_second_ref[f])
        first = jnp.where(low_half, below, shift(above, 64))
        second = jnp.where(low_half, shift(below, 64), above)
        ends_ref[f, 0] = first
        ends_ref[f, 1] = second
        x_first_ref[f, 8], x_second_ref[f, 8] = give(even_x, first, second)
        for n in range(8):
            x_first_ref[f, n], x_second_ref[f, n] = give(even_x, fields_ref[f, n], fields_ref[f, 8 + n])


def pack_y_kernel(place_ref, fields_ref, ends_ref, x_first_ref, x_second_ref, y_first_ref, y_second_ref):
    even_x, even_y = place_ref[4] == 0, place_ref[5] == 0

    def put(f, plane, value):
        y_first_ref[f, plane], y_second_ref[f, plane] = give(even_y, value[0:8], value[8:16])

    for f in range(fields_ref.shape[0]):
        for n in range(16):
            put(f, n, fields_ref[f, n])
        for n in range(9):
            low, high = take(even_x, x_first_ref[f, n], x_second_ref[f, n])
            put(f, 16 + n, low)
            put(f, 25 + n, high)
        for n in range(2):
            put(f, 34 + n, ends_ref[f, n])


def exchange(place, fields, z_first, z_second, before=()):
    count = fields.shape[0]
    z_first, z_second = trade(z_first, z_second, "gz")
    x_first, x_second, ends = pl.pallas_call(
        pack_x_kernel,
        in_specs=[SMEM] + [VMEM] * 3 + [HBM] * len(before),
        out_specs=[VMEM] * 3,
        out_shape=[shape(count, 9, 16, 128), shape(count, 9, 16, 128), shape(count, 2, 16, 128)],
        compiler_params=params(8),
        cost_estimate=LONG,
        name="pack_x",
    )(place, fields, z_first, z_second, *in_hbm(*before))
    x_first, x_second = trade(x_first, x_second, "gx")
    y_first, y_second = pl.pallas_call(
        pack_y_kernel,
        in_specs=[SMEM] + [VMEM] * 4,
        out_specs=[VMEM] * 2,
        out_shape=[shape(count, 36, 8, 128)] * 2,
        compiler_params=params(8),
        cost_estimate=LONG,
        name="pack_y",
    )(place, fields, ends, x_first, x_second)
    y_first, y_second = trade(y_first, y_second, "gy")
    return fields, ends, x_first, x_second, y_first, y_second


def shape(*dims, dtype=f32):
    return jax.ShapeDtypeStruct(dims, dtype)


def wide_scratch(count):
    return [pltpu.VMEM((8, ROWS, 128), f32) for _ in range(count)]


def work_scratch():
    return wide_scratch(12)


def on_device(
    electrolyte,
    conductivity,
    phase_label,
    applied_current,
    slot_count,
    slot_cell,
    slot_label,
    slot_area,
    slot_rate,
    owner_map,
    shell_count,
    shell_conc,
    shell_inverse,
):
    size_x, size_y, size_z = (lax.axis_size(a) for a in ("gx", "gy", "gz"))
    at = [lax.axis_index(a) for a in ("gx", "gy", "gz")]
    place = jnp.stack(at[:2] + [size_x, size_y] + [a % 2 for a in at]).astype(jnp.int32)
    cell = slot_cell.reshape(16, 128)
    shells = shell_count.reshape(1, 128)
    conc = shell_conc.reshape(64, 128)
    given = (
        cell,
        slot_label.reshape(16, 128),
        owner_map.reshape(8, 128),
        slot_area.reshape(16, 128),
        slot_rate.reshape(16, 128),
        electrolyte,
        conductivity,
        phase_label,
        shells,
        conc,
    )
    fields, z_first, z_second, column, position = pl.pallas_call(
        prepare_kernel,
        in_specs=[SMEM] * 2 + [HBM] * 10,
        out_specs=[VMEM] * 5,
        out_shape=[
            shape(4, 16, 16, 128),
            shape(4, 16, 128),
            shape(4, 16, 128),
            shape(8, 16, 128),
            shape(16, 128, dtype=jnp.int32),
        ],
        scratch_shapes=[
            pltpu.VMEM((8, 128), f32),
            pltpu.VMEM((256, 2048), bf16),
            pltpu.VMEM((512, 2048), bf16),
            pltpu.VMEM((48, 2048), bf16),
            pltpu.VMEM((128, 2048), bf16),
        ]
        + [pltpu.VMEM(array.shape, array.dtype) for array in given]
        + [pltpu.SemaphoreType.DMA((len(given),))],
        compiler_params=params(12),
        name="prepare",
    )(place, slot_count, *in_hbm(*given))
    column = lax.all_to_all(column, "gz", 0, 0, tiled=True)
    pieces = exchange(place, fields, z_first, z_second, (column,))
    sums = pl.pallas_call(
        column_kernel,
        in_specs=[VMEM],
        out_specs=VMEM,
        out_shape=shape(size_x * size_y, SUM_ROWS, 128),
        compiler_params=params(4),
        name="column",
    )(column)
    sums = lax.all_to_all(sums, ("gx", "gy"), 0, 0, tiled=True)
    wide = shape(8, ROWS, 128)
    devices = size_x * size_y * size_z
    start, k, w, circuit, fields, z_first, z_second, part, state = pl.pallas_call(
        first_kernel,
        in_specs=[SMEM] * 2 + [VMEM] * 7,
        out_specs=[HBM] * 4 + [VMEM] * 5,
        out_shape=[
            *[pltpu.HBM(wide.shape, f32)] * 4,
            shape(2, 16, 16, 128),
            shape(2, 16, 128),
            shape(2, 16, 128),
            shape(devices, PART_ROWS, 128),
            shape(8, 128),
        ],
        scratch_shapes=wide_scratch(4)
        + [pltpu.SemaphoreType.DMA((4,))]
        + wide_scratch(1)
        + [pltpu.VMEM((9, 8, 128), f32)]
        + work_scratch(),
        compiler_params=params(),
        name="first_sweep",
    )(place, applied_current, *pieces, sums)
    pieces = exchange(place, fields, z_first, z_second)
    part = lax.all_to_all(part, ("gx", "gy", "gz"), 0, 0, tiled=True)
    concentration, potential, flux = pl.pallas_call(
        second_kernel,
        in_specs=[SMEM] * 2 + [VMEM] * 10 + [HBM] * 4,
        out_specs=[VMEM] * 3,
        out_shape=[shape(16, 16, 128), shape(16, 16, 128), shape(8, 128)],
        scratch_shapes=wide_scratch(4)
        + [pltpu.SemaphoreType.DMA((4,))]
        + wide_scratch(2)
        + [pltpu.VMEM((256, 128), f32), pltpu.VMEM((256, 2048), bf16)]
        + [pltpu.VMEM((48, 2048), bf16), pltpu.VMEM((128, 2048), bf16)]
        + work_scratch(),
        compiler_params=params(),
        name="second_sweep",
    )(place, applied_current, *pieces, part, state, cell, position, *in_hbm(start, k, w, circuit))
    base, surface_column = pl.pallas_call(
        shell_kernel,
        grid=(8,),
        in_specs=[
            pl.BlockSpec((8, 64, 128), lambda i: (i, 0, 0)),
            pl.BlockSpec((1, 128), lambda i: (0, 0)),
            pl.BlockSpec((64, 128), lambda i: (0, 0)),
        ],
        out_specs=[pl.BlockSpec((8, 128), lambda i: (i, 0))] * 2,
        out_shape=[shape(64, 128)] * 2,
        compiler_params=params(8),
        name="shells",
    )(shell_inverse.reshape(64, 64, 128), shells, conc)
    flux = jnp.sum(lax.all_to_all(flux, "gz", 0, 0, tiled=True), axis=0, keepdims=True)
    updated = base + shell_step * flux * surface_column
    return (concentration, potential, updated[None, None])


def solution(mesh):
    placed = (
        P("gx", "gy", "gz"),
        P("gx", "gy", "gz"),
        P("gx", "gy", "gz"),
        P(),
        P("gx", "gy", "gz"),
        P("gx", "gy", "gz"),
        P("gx", "gy", "gz"),
        P("gx", "gy", "gz"),
        P("gx", "gy", "gz"),
        P("gx", "gy", None),
        P("gx", "gy", "gz"),
        P("gx", "gy", None, "gz"),
        P("gx", "gy", None, None, "gz"),
    )
    return jax.shard_map(
        on_device,
        mesh=mesh,
        in_specs=placed,
        out_specs=(P("gx", "gy", "gz"), P("gx", "gy", "gz"), P("gx", "gy", None, "gz")),
        check_vma=False,
    )
```

```python
import functools

import jax
import jax.numpy as jnp
from jax import lax
from jax.experimental import pallas as pl
from jax.experimental.pallas import tpu as pltpu
from jax.sharding import PartitionSpec as P

SWEEPS = 2
ITERS = 8

inv_step = 4.0
conc_coupling = 0.5
solid_factor = 0.1
shell_step = 0.02

ROWS = 160
FIRST = 16
TILES = 18
UNROLL = 18
PART_ROWS = 2
SUM_ROWS = 16
SETUP = 6
LAST = 4
f32 = jnp.float32
bf16 = jnp.bfloat16
VMEM = pl.BlockSpec(memory_space=pltpu.VMEM)
SMEM = pl.BlockSpec(memory_space=pltpu.SMEM)
HBM = pl.BlockSpec(memory_space=pltpu.HBM)


LONG = pl.CostEstimate(flops=0, bytes_accessed=160 * 1024 * 1024, transcendentals=0)


def params(mebibytes=24):
    return pltpu.CompilerParams(vmem_limit_bytes=mebibytes * 1024 * 1024)


def in_hbm(*arrays):
    return [pltpu.with_memory_space_constraint(array, pltpu.HBM) for array in arrays]


def copies(sources, targets, sems):
    return [pltpu.make_async_copy(s, t, sems.at[n]) for n, (s, t) in enumerate(zip(sources, targets))]


def iota(shape, dim):
    return lax.broadcasted_iota(jnp.int32, shape, dim)


def lookup(table_ref, rows, low, high, init):
    value = init
    for row in range(rows):
        line = jnp.broadcast_to(table_ref[pl.ds(row, 1), :], (8, 128))
        found = jnp.take_along_axis(line, low, axis=1)
        value = found if row == 0 else jnp.where(high == row, found, value)
    return value


def split_value(value, pieces):
    out = []
    for _ in range(pieces):
        part = value.astype(bf16).astype(f32)
        out.append(part)
        value = value - part
    return out


def by_particle(value, position, left_ref, right_ref):
    parts = split_value(value, 3)
    low = jnp.bitwise_and(position, 127)
    high = jnp.right_shift(position, 7)
    row_high = iota((16, 128), 0)
    row_low = iota((128, 128), 0)
    for t in range(16):
        mask = row_high == high[t : t + 1]
        for n, part in enumerate(parts):
            left_ref[16 * n : 16 * n + 16, 128 * t : 128 * t + 128] = jnp.where(mask, part[t : t + 1], 0.0).astype(bf16)
        right_ref[:, 128 * t : 128 * t + 128] = jnp.where(row_low == low[t : t + 1], 1.0, 0.0).astype(bf16)
    total = lax.dot_general(left_ref[...], right_ref[...], (((1,), (1,)), ((), ())), preferred_element_type=f32)
    return total[0:8] + total[16:24] + total[32:40]


def mark_rows(cell, high_ref):
    high = jnp.right_shift(cell, 7)
    row = iota((256, 128), 0)
    for t in range(16):
        high_ref[:, 128 * t : 128 * t + 128] = jnp.where(row == high[t : t + 1], 1.0, 0.0).astype(bf16)


def sample(flat, cell, high_ref):
    parts = split_value(flat.T, 2)
    left = jnp.concatenate(parts, axis=0).astype(bf16)
    low = jnp.bitwise_and(cell, 127)
    row = iota((128, 128), 0)
    out = []
    for t in range(0, 16, 2):
        found = jnp.dot(left, high_ref[:, 128 * t : 128 * t + 256], preferred_element_type=f32)
        found = found[0:128] + found[128:256]
        for u in range(2):
            mask = row == low[t + u : t + u + 1]
            out.append(jnp.sum(jnp.where(mask, found[:, 128 * u : 128 * u + 128], 0.0), axis=0, keepdims=True))
    return jnp.concatenate(out, axis=0)


def open_circuit(surface_conc):
    return 0.4 * jnp.tanh(3.0 * (0.5 - surface_conc))


def prepare_kernel(
    place_ref,
    count_ref,
    cell_hbm,
    label_hbm,
    owner_hbm,
    area_hbm,
    rate_hbm,
    conc_hbm,
    cond_hbm,
    phase_hbm,
    shells_hbm,
    shell_conc_hbm,
    fields_ref,
    z_first_ref,
    z_second_ref,
    column_ref,
    position_ref,
    owner_f_ref,
    high_ref,
    value_ref,
    left_ref,
    right_ref,
    cell_ref,
    label_ref,
    owner_ref,
    area_ref,
    rate_ref,
    conc_ref,
    cond_ref,
    phase_ref,
    shells_ref,
    shell_conc_ref,
    sems,
):
    held = (cell_ref, label_ref, owner_ref, area_ref, rate_ref, conc_ref, cond_ref, phase_ref, shells_ref, shell_conc_ref)
    given = (cell_hbm, label_hbm, owner_hbm, area_hbm, rate_hbm, conc_hbm, cond_hbm, phase_hbm, shells_hbm, shell_conc_hbm)
    reads = copies(given, held, sems)
    for read in reads:
        read.start()
    for read in reads:
        read.wait()
    lane = iota((16, 128), 1)
    slot = iota((16, 128), 0) * 128 + lane
    live = (slot < count_ref[0, 0, 0]).astype(f32)
    label = label_ref[...]
    owner_f_ref[...] = owner_ref[...].astype(f32)
    low = jnp.bitwise_and(label, 127)
    high = jnp.right_shift(label, 7)
    position = jnp.concatenate(
        [lookup(owner_f_ref, 8, low[h : h + 8], high[h : h + 8], None) for h in (0, 8)], axis=0
    ).astype(jnp.int32)
    position_ref[...] = position
    area = area_ref[...]
    weight = live * area * rate_ref[...]
    cell = cell_ref[...]
    cell_low = jnp.bitwise_and(cell, 127)
    mark_rows(cell, high_ref)

    parts = split_value(weight, 2) + [
        jnp.right_shift(position, 3).astype(f32),
        jnp.bitwise_and(position, 7).astype(f32),
    ]
    row_low = iota((128, 128), 0)
    for t in range(16):
        columns = slice(128 * t, 128 * t + 128)
        mask = row_low == cell_low[t : t + 1]
        for n, part in enumerate(parts):
            value_ref[128 * n : 128 * n + 128, columns] = jnp.where(mask, part[t : t + 1], 0.0).astype(bf16)
    dense = lax.dot_general(high_ref[...], value_ref[...], (((1,), (1,)), ((), ())), preferred_element_type=f32)
    fields_ref[0] = conc_ref[...]
    fields_ref[1] = cond_ref[...] * jnp.where(phase_ref[...] == 1, solid_factor, 1.0)
    fields_ref[2] = (dense[:, 0:128] + dense[:, 128:256]).reshape(16, 16, 128)
    fields_ref[3] = (dense[:, 256:384] * 8.0 + dense[:, 384:512]).reshape(16, 16, 128)

    for f in range(4):
        z_low = jnp.zeros((16, 128), f32)
        z_high = jnp.zeros((16, 128), f32)
        for x in range(16):
            plane = fields_ref[f, x]
            mask = jnp.right_shift(lane, 3) == x
            z_low = jnp.where(mask, pltpu.roll(plane, 8 * x, 1) if x else plane, z_low)
            z_high = jnp.where(mask, pltpu.roll(plane, (8 * x + 8) % 128, 1) if x < 15 else plane, z_high)
        z_first_ref[f], z_second_ref[f] = give(place_ref[6] == 0, z_low, z_high)

    sampled = sample(conc_ref[...].reshape(256, 128), cell, high_ref)
    summed = by_particle(weight * (1.0 + 0.5 * jnp.tanh(sampled)), position, left_ref, right_ref)
    surface_shell = iota((64, 128), 0) == shells_ref[...] - 1
    surface = jnp.sum(jnp.where(surface_shell, shell_conc_ref[...], 0.0), axis=0, keepdims=True)
    area_sum = jnp.sum(live * area, axis=0, keepdims=True)
    tail = jnp.concatenate([surface, area_sum, jnp.zeros((6, 128), f32)], axis=0)
    block = jnp.concatenate([summed, tail], axis=0)
    for n in range(8):
        column_ref[n] = block


def column_kernel(column_ref, sums_ref):
    weight = jnp.zeros((8, 128), f32)
    area = jnp.zeros((1, 128), f32)
    for n in range(8):
        weight = weight + column_ref[n, 0:8]
        area = area + column_ref[n, 9:10]
    surface = jnp.concatenate([column_ref[n, 8:9] for n in range(8)], axis=0)
    circuit = open_circuit(surface)
    growth = jnp.exp(-0.5 * circuit)
    shrink = jnp.exp(0.5 * circuit)
    current = jnp.sum(weight * (growth - shrink), axis=0, keepdims=True)
    slope = jnp.sum(weight * (0.5 * (growth + shrink)), axis=0, keepdims=True)
    block = jnp.concatenate([circuit, current, slope, area, jnp.zeros((5, 128), f32)], axis=0)
    for n in range(sums_ref.shape[0]):
        sums_ref[n, 0:16] = block


def total_of(value):
    return jnp.sum(jnp.sum(value, axis=0, keepdims=True), axis=1, keepdims=True)


def shift(value, by):
    return pltpu.roll(value, by % 128, 1)


def widen(load, wide_ref):
    def square(planes):
        return jnp.concatenate([load(p, t) for p in planes for t in range(4)], axis=0).T

    for n in range(8):
        wide_ref[n, FIRST : FIRST + 128] = square((16 + n, n, 8 + n, 25 + n))
    ends = square((24, 34, 35, 33))
    for n in range(8):
        wide_ref[n, FIRST - 8 : FIRST] = ends[8 * n : 8 * n + 8]
        wide_ref[n, FIRST + 128 : FIRST + 136] = ends[64 + 8 * n : 72 + 8 * n]
        wide_ref[n, 0 : FIRST - 8] = jnp.zeros((8, 128), f32)
        wide_ref[n, FIRST + 136 : ROWS] = jnp.zeros((8, 128), f32)


def loader(f, place_ref, centre_ref, ends_ref, x_first_ref, x_second_ref, y_first_ref, y_second_ref):
    even_x, even_y = place_ref[4] == 0, place_ref[5] == 0

    def load(plane, tile):
        if tile in (0, 3):
            return take(even_y, y_first_ref[f, plane], y_second_ref[f, plane])[tile // 3]
        rows = slice(8 * tile - 8, 8 * tile)
        if plane < 16:
            return centre_ref[f, plane, rows]
        if plane < 34:
            side, n = divmod(plane - 16, 9)
            return take(even_x, x_first_ref[f, n, rows], x_second_ref[f, n, rows])[side]
        return ends_ref[f, plane - 34, rows]

    return load


def narrow(wide_ref, store):
    for n in range(8):
        square = wide_ref[n, FIRST : FIRST + 128].T
        store(n, square[40:56])
        store(8 + n, square[72:88])


def end_slabs(wide_ref):
    square = jnp.concatenate(
        [wide_ref[n, FIRST : FIRST + 8] for n in range(8)]
        + [wide_ref[n, FIRST + 120 : FIRST + 128] for n in range(8)],
        axis=0,
    ).T
    first, second = square[40:56], square[72:88]
    low_half = iota((16, 128), 1) < 64
    low = jnp.where(low_half, first, shift(second, 64))
    high = jnp.where(low_half, shift(first, 64), second)
    return low, high


def tiles(body, first=0, last=TILES, unroll=1):
    def step(n, carry):
        body(pl.multiple_of(8 + 8 * n, 8))
        return carry

    lax.fori_loop(first, last, step, 0, unroll=unroll)


def solve(c_ref, p_ref, start_ref, k_ref, w_ref, circuit_ref, solid, work):
    fx, fy, fz, rc, rp, gc, gp, coup, dc, dp, dc_next, dp_next = work

    def set_faces(r):
        k = [k_ref[n, pl.ds(r, 8)] for n in range(8)]
        for n in range(8):
            below = k[n - 1] if n else shift(k[7], 32)
            fx[n, pl.ds(r, 8)] = 0.5 * (k[n] + below)
            fy[n, pl.ds(r, 8)] = 0.5 * (k[n] + shift(k[n], 1))
            fz[n, pl.ds(r, 8)] = 0.5 * (k[n] + k_ref[n, pl.ds(r - 1, 8)])

    for n in range(8):
        fz[n, FIRST + 136 : ROWS] = jnp.zeros((8, 128), f32)
        for ref in (dc, dp, dc_next, dp_next):
            ref[n, 0 : FIRST - 8] = jnp.zeros((8, 128), f32)
            ref[n, FIRST + 136 : ROWS] = jnp.zeros((8, 128), f32)
    tiles(set_faces, unroll=SETUP)

    def faces(r):
        lower = [fx[n, pl.ds(r, 8)] for n in range(8)]
        return lower + [shift(lower[0], -32)]

    def beside(values, n, source, r, x_faces, y_face, z_face, z_next):
        low = values[n - 1] if n else shift(values[7], 32)
        high = values[n + 1] if n < 7 else shift(values[0], -32)
        total = x_faces[n] * low + x_faces[n + 1] * high
        total = total + (y_face * shift(values[n], 1) + shift(y_face * values[n], -1))
        return total + (z_face * source[n, pl.ds(r - 1, 8)] + z_next * source[n, pl.ds(r + 1, 8)])

    def set_system(r):
        rows = pl.ds(r, 8)
        c = [c_ref[n, rows] for n in range(8)]
        p = None if p_ref is None else [p_ref[n, rows] for n in range(8)]
        x_faces = faces(r)
        for n in range(8):
            y_face, z_face, z_next = fy[n, rows], fz[n, rows], fz[n, pl.ds(r + 1, 8)]
            face_total = x_faces[n] + x_faces[n + 1] + y_face + shift(y_face, -1) + z_face + z_next
            over = solid - circuit_ref[n, rows]
            if p is not None:
                over = over - p[n]
            growth = jnp.exp(0.5 * over)
            shrink = jnp.exp(-0.5 * over)
            factor = w_ref[n, rows] * (1.0 + 0.5 * jnp.tanh(c[n]))
            source = factor * (growth - shrink)
            uptake = factor * (0.5 * (growth + shrink))
            rhs_c = beside(c, n, c_ref, r, x_faces, y_face, z_face, z_next) - face_total * c[n] - conc_coupling * source
            rhs_p = source
            if p is not None:
                rhs_c = rhs_c - (c[n] - start_ref[n, rows]) * inv_step
                rhs_p = rhs_p + (beside(p, n, p_ref, r, x_faces, y_face, z_face, z_next) - face_total * p[n])
            inside = k_ref[n, rows] > 0.0
            recip_c = jnp.where(inside, 1.0 / (inv_step + face_total), 0.0)
            recip_p = jnp.where(inside, 1.0 / (face_total + uptake), 0.0)
            rc[n, rows] = rhs_c
            rp[n, rows] = rhs_p
            gc[n, rows] = recip_c
            gp[n, rows] = recip_p
            coup[n, rows] = conc_coupling * uptake
            dc[n, rows] = rhs_c * recip_c
            dp[n, rows] = rhs_p * recip_p

    tiles(set_system, unroll=SETUP)

    def iteration(c_now, p_now, c_then, p_then):
        def relax(r):
            rows = pl.ds(r, 8)
            c = [c_now[n, rows] for n in range(8)]
            p = [p_now[n, rows] for n in range(8)]
            x_faces = faces(r)
            for n in range(8):
                y_face, z_face, z_next = fy[n, rows], fz[n, rows], fz[n, pl.ds(r + 1, 8)]
                next_c = beside(c, n, c_now, r, x_faces, y_face, z_face, z_next)
                next_p = beside(p, n, p_now, r, x_faces, y_face, z_face, z_next)
                c_then[n, rows] = (rc[n, rows] + next_c + coup[n, rows] * p[n]) * gc[n, rows]
                p_then[n, rows] = (rp[n, rows] + next_p) * gp[n, rows]

        tiles(relax, unroll=UNROLL)

    def pair(_, carry):
        iteration(dc, dp, dc_next, dp_next)
        iteration(dc_next, dp_next, dc, dp)
        return carry

    lax.fori_loop(0, (ITERS - 1) // 2, pair, 0)
    if ITERS % 2 == 0:
        iteration(dc, dp, dc_next, dp_next)
        return dc_next, dp_next
    return dc, dp


def first_kernel(
    place_ref,
    current_ref,
    centre_ref,
    ends_ref,
    x_first_ref,
    x_second_ref,
    y_first_ref,
    y_second_ref,
    sums_ref,
    start_hbm,
    k_hbm,
    w_hbm,
    circuit_hbm,
    fields_ref,
    z_first_ref,
    z_second_ref,
    part_ref,
    state_ref,
    start_ref,
    k_ref,
    w_ref,
    circuit_ref,
    sems,
    c_ref,
    table_ref,
    *work,
):
    writes = copies((start_ref, k_ref, w_ref, circuit_ref), (start_hbm, k_hbm, w_hbm, circuit_hbm), sems)
    pieces = (place_ref, centre_ref, ends_ref, x_first_ref, x_second_ref, y_first_ref, y_second_ref)
    widen(loader(0, *pieces), start_ref)
    widen(loader(1, *pieces), k_ref)
    widen(loader(2, *pieces), w_ref)
    at_x, at_y, size_x, size_y = place_ref[0], place_ref[1], place_ref[2], place_ref[3]
    for i in range(3):
        for j in range(3):
            near_x = jnp.clip(at_x + (i - 1), 0, size_x - 1)
            near_y = jnp.clip(at_y + (j - 1), 0, size_y - 1)
            table_ref[3 * i + j] = sums_ref[near_x * size_y + near_y, 0:8]
    positions = loader(3, *pieces)

    def circuit(plane, tile):
        i = 0 if 16 <= plane < 25 else 2 if 25 <= plane < 34 else 1
        j = (0, 1, 1, 2)[tile]
        position = positions(plane, tile).astype(jnp.int32)
        return lookup(
            table_ref.at[3 * i + j], 8, jnp.bitwise_and(position, 127), jnp.right_shift(position, 7), None
        )

    widen(circuit, circuit_ref)
    for write in writes:
        write.start()

    sums = sums_ref[0, 8:16]
    for n in range(1, sums_ref.shape[0]):
        sums = sums + sums_ref[n, 8:16]
    sums = jnp.sum(sums, axis=1, keepdims=True)
    current, slope, area = sums[0:1], sums[1:2], sums[2:3]
    solid = (current_ref[0] * area - current) / slope
    dc, dp = solve(start_ref, None, start_ref, k_ref, w_ref, circuit_ref, solid, work)

    lane = iota((8, 128), 1)
    mine = (lane >= 32) & (lane < 96) & (lane % 32 >= 8) & (lane % 32 < 24)
    zero = jnp.zeros((8, 128), f32)

    def finish(n, carry):
        rows = pl.ds(pl.multiple_of(8 + 8 * n, 8), 8)
        total, weight = carry
        for m in range(8):
            c = start_ref[m, rows] + dc[m, rows]
            p = dp[m, rows]
            c_ref[m, rows] = c
            over = solid - p - circuit_ref[m, rows]
            growth = jnp.exp(0.5 * over)
            shrink = jnp.exp(-0.5 * over)
            factor = w_ref[m, rows] * (1.0 + 0.5 * jnp.tanh(c))
            total = total + factor * (growth - shrink)
            weight = weight + factor * (0.5 * (growth + shrink))
        return total, weight

    total, weight = lax.fori_loop(1, TILES - 1, finish, (zero, zero), unroll=LAST)
    total = total_of(jnp.where(mine, total, 0.0))
    weight = total_of(jnp.where(mine, weight, 0.0))
    row = iota((8, 128), 1)
    block = jnp.where(row == 0, total, jnp.where(row == 1, weight, 0.0))

    def spread(n, carry):
        part_ref[n] = block[: part_ref.shape[1]]
        return carry

    lax.fori_loop(0, part_ref.shape[0], spread, 0, unroll=8)
    state_ref[...] = jnp.where(row == 0, solid, jnp.where(row == 1, area, 0.0))
    for f, ref in enumerate((c_ref, dp)):

        def store(plane, value, f=f):
            fields_ref[f, plane] = value

        narrow(ref, store)
        z_first_ref[f], z_second_ref[f] = give(place_ref[6] == 0, *end_slabs(ref))
    for write in writes:
        write.wait()


def second_kernel(
    place_ref,
    current_ref,
    centre_ref,
    ends_ref,
    x_first_ref,
    x_second_ref,
    y_first_ref,
    y_second_ref,
    part_ref,
    state_ref,
    cell_ref,
    position_ref,
    start_hbm,
    k_hbm,
    w_hbm,
    circuit_hbm,
    conc_ref,
    pot_ref,
    flux_ref,
    start_ref,
    k_ref,
    w_ref,
    circuit_ref,
    sems,
    c_ref,
    p_ref,
    flat_ref,
    high_ref,
    left_ref,
    right_ref,
    *work,
):
    pieces = (place_ref, centre_ref, ends_ref, x_first_ref, x_second_ref, y_first_ref, y_second_ref)
    reads = copies((start_hbm, k_hbm, w_hbm, circuit_hbm), (start_ref, k_ref, w_ref, circuit_ref), sems)
    for read in reads:
        read.start()
    widen(loader(0, *pieces), c_ref)
    widen(loader(1, *pieces), p_ref)
    for read in reads:
        read.wait()
    sums = part_ref[0]
    for n in range(1, part_ref.shape[0]):
        sums = sums + part_ref[n]
    sums = sums[0:1]
    current, slope = sums[:, 0:1], sums[:, 1:2]
    before, area = state_ref[0:1, 0:1], state_ref[0:1, 1:2]
    solid = before + (current_ref[0] * area - current) / slope
    dc, dp = solve(c_ref, p_ref, start_ref, k_ref, w_ref, circuit_ref, solid, work)
    flux = work[0]

    def finish(r):
        rows = pl.ds(r, 8)
        for m in range(8):
            c = c_ref[m, rows] + dc[m, rows]
            p = p_ref[m, rows] + dp[m, rows]
            c_ref[m, rows] = c
            p_ref[m, rows] = p
            over = solid - p - circuit_ref[m, rows]
            factor = w_ref[m, rows] * (1.0 + 0.5 * jnp.tanh(c))
            flux[m, rows] = factor * (jnp.exp(0.5 * over) - jnp.exp(-0.5 * over))

    tiles(finish, 1, TILES - 1, unroll=LAST)

    def store_conc(plane, value):
        conc_ref[plane] = value

    def store_pot(plane, value):
        pot_ref[plane] = value

    def store_flux(plane, value):
        flat_ref[16 * plane : 16 * plane + 16] = value

    narrow(flux, store_flux)
    cell = cell_ref[...]
    mark_rows(cell, high_ref)
    sampled = sample(flat_ref[...], cell, high_ref)
    flux_ref[...] = by_particle(sampled, position_ref[...], left_ref, right_ref)
    narrow(c_ref, store_conc)
    narrow(p_ref, store_pot)


def shell_kernel(inverse_ref, shells_ref, conc_ref, base_ref, column_ref):
    count = shells_ref[...]
    index = iota((64, 128), 0)
    fill = (index < count).astype(f32)
    surface = index == count - 1
    load = conc_ref[...] * fill
    rows = inverse_ref.shape[0]
    base, column = [], []
    for i in range(rows):
        matrix = inverse_ref[i]
        base.append(jnp.sum(matrix * load, axis=0, keepdims=True))
        column.append(jnp.sum(jnp.where(surface, matrix, 0.0), axis=0, keepdims=True))
    keep = (iota((rows, 128), 0) + pl.program_id(0) * rows < count).astype(f32)
    base_ref[...] = jnp.concatenate(base, axis=0) * keep
    column_ref[...] = jnp.concatenate(column, axis=0) * keep


def trade(first, second, axis):
    count = lax.axis_size(axis)
    pairs = [(i, i ^ 1) for i in range(count)]
    others = [(i, i + 1) for i in range(1, count - 1, 2)]
    others = others + [(target, source) for source, target in others]
    return lax.ppermute(first, axis, pairs), lax.ppermute(second, axis, others)


def give(even, low, high):
    return jnp.where(even, high, low), jnp.where(even, low, high)


def take(even, first, second):
    return jnp.where(even, second, first), jnp.where(even, first, second)


def pack_x_kernel(place_ref, fields_ref, z_first_ref, z_second_ref, *rest):
    x_first_ref, x_second_ref, ends_ref = rest[-3:]
    even_x, even_z = place_ref[4] == 0, place_ref[6] == 0
    low_half = iota((16, 128), 1) < 64
    for f in range(fields_ref.shape[0]):
        below, above = take(even_z, z_first_ref[f], z_second_ref[f])
        first = jnp.where(low_half, below, shift(above, 64))
        second = jnp.where(low_half, shift(below, 64), above)
        ends_ref[f, 0] = first
        ends_ref[f, 1] = second
        x_first_ref[f, 8], x_second_ref[f, 8] = give(even_x, first, second)
        for n in range(8):
            x_first_ref[f, n], x_second_ref[f, n] = give(even_x, fields_ref[f, n], fields_ref[f, 8 + n])


def pack_y_kernel(place_ref, fields_ref, ends_ref, x_first_ref, x_second_ref, *rest):
    y_first_ref, y_second_ref = rest[-2:]
    even_x, even_y = place_ref[4] == 0, place_ref[5] == 0

    def put(f, plane, value):
        y_first_ref[f, plane], y_second_ref[f, plane] = give(even_y, value[0:8], value[8:16])

    for f in range(fields_ref.shape[0]):
        for n in range(16):
            put(f, n, fields_ref[f, n])
        for n in range(9):
            low, high = take(even_x, x_first_ref[f, n], x_second_ref[f, n])
            put(f, 16 + n, low)
            put(f, 25 + n, high)
        for n in range(2):
            put(f, 34 + n, ends_ref[f, n])


def exchange(place, fields, z_first, z_second, before_x=(), before_y=()):
    count = fields.shape[0]
    z_first, z_second = trade(z_first, z_second, "gz")
    x_first, x_second, ends = pl.pallas_call(
        pack_x_kernel,
        in_specs=[SMEM] + [VMEM] * 3 + [HBM] * len(before_x),
        out_specs=[VMEM] * 3,
        out_shape=[shape(count, 9, 16, 128), shape(count, 9, 16, 128), shape(count, 2, 16, 128)],
        compiler_params=params(8),
        cost_estimate=LONG,
        name="pack_x",
    )(place, fields, z_first, z_second, *in_hbm(*before_x))
    x_first, x_second = trade(x_first, x_second, "gx")
    y_first, y_second = pl.pallas_call(
        pack_y_kernel,
        in_specs=[SMEM] + [VMEM] * 4 + [HBM] * len(before_y),
        out_specs=[VMEM] * 2,
        out_shape=[shape(count, 36, 8, 128)] * 2,
        compiler_params=params(8),
        cost_estimate=LONG,
        name="pack_y",
    )(place, fields, ends, x_first, x_second, *in_hbm(*before_y))
    y_first, y_second = trade(y_first, y_second, "gy")
    return fields, ends, x_first, x_second, y_first, y_second


def shape(*dims, dtype=f32):
    return jax.ShapeDtypeStruct(dims, dtype)


def wide_scratch(count):
    return [pltpu.VMEM((8, ROWS, 128), f32) for _ in range(count)]


def work_scratch():
    return wide_scratch(12)


def on_device(
    electrolyte,
    conductivity,
    phase_label,
    applied_current,
    slot_count,
    slot_cell,
    slot_label,
    slot_area,
    slot_rate,
    owner_map,
    shell_count,
    shell_conc,
    shell_inverse,
):
    size_x, size_y, size_z = (lax.axis_size(a) for a in ("gx", "gy", "gz"))
    at = [lax.axis_index(a) for a in ("gx", "gy", "gz")]
    place = jnp.stack(at[:2] + [size_x, size_y] + [a % 2 for a in at]).astype(jnp.int32)
    cell = slot_cell.reshape(16, 128)
    shells = shell_count.reshape(1, 128)
    conc = shell_conc.reshape(64, 128)
    given = (
        cell,
        slot_label.reshape(16, 128),
        owner_map.reshape(8, 128),
        slot_area.reshape(16, 128),
        slot_rate.reshape(16, 128),
        electrolyte,
        conductivity,
        phase_label,
        shells,
        conc,
    )
    fields, z_first, z_second, column, position = pl.pallas_call(
        prepare_kernel,
        in_specs=[SMEM] * 2 + [HBM] * 10,
        out_specs=[VMEM] * 5,
        out_shape=[
            shape(4, 16, 16, 128),
            shape(4, 16, 128),
            shape(4, 16, 128),
            shape(8, 16, 128),
            shape(16, 128, dtype=jnp.int32),
        ],
        scratch_shapes=[
            pltpu.VMEM((8, 128), f32),
            pltpu.VMEM((256, 2048), bf16),
            pltpu.VMEM((512, 2048), bf16),
            pltpu.VMEM((48, 2048), bf16),
            pltpu.VMEM((128, 2048), bf16),
        ]
        + [pltpu.VMEM(array.shape, array.dtype) for array in given]
        + [pltpu.SemaphoreType.DMA((len(given),))],
        compiler_params=params(12),
        name="prepare",
    )(place, slot_count, *in_hbm(*given))
    column = lax.all_to_all(column, "gz", 0, 0, tiled=True)
    sums = pl.pallas_call(
        column_kernel,
        in_specs=[VMEM],
        out_specs=VMEM,
        out_shape=shape(size_x * size_y, SUM_ROWS, 128),
        compiler_params=params(4),
        name="column",
    )(column)
    pieces = exchange(place, fields, z_first, z_second, (column,), (sums,))
    sums = lax.all_to_all(sums, ("gx", "gy"), 0, 0, tiled=True)
    wide = shape(8, ROWS, 128)
    devices = size_x * size_y * size_z
    start, k, w, circuit, fields, z_first, z_second, part, state = pl.pallas_call(
        first_kernel,
        in_specs=[SMEM] * 2 + [VMEM] * 7,
        out_specs=[HBM] * 4 + [VMEM] * 5,
        out_shape=[
            *[pltpu.HBM(wide.shape, f32)] * 4,
            shape(2, 16, 16, 128),
            shape(2, 16, 128),
            shape(2, 16, 128),
            shape(devices, PART_ROWS, 128),
            shape(8, 128),
        ],
        scratch_shapes=wide_scratch(4)
        + [pltpu.SemaphoreType.DMA((4,))]
        + wide_scratch(1)
        + [pltpu.VMEM((9, 8, 128), f32)]
        + work_scratch(),
        compiler_params=params(),
        name="first_sweep",
    )(place, applied_current, *pieces, sums)
    pieces = exchange(place, fields, z_first, z_second)
    part = lax.all_to_all(part, ("gx", "gy", "gz"), 0, 0, tiled=True)
    concentration, potential, flux = pl.pallas_call(
        second_kernel,
        in_specs=[SMEM] * 2 + [VMEM] * 10 + [HBM] * 4,
        out_specs=[VMEM] * 3,
        out_shape=[shape(16, 16, 128), shape(16, 16, 128), shape(8, 128)],
        scratch_shapes=wide_scratch(4)
        + [pltpu.SemaphoreType.DMA((4,))]
        + wide_scratch(2)
        + [pltpu.VMEM((256, 128), f32), pltpu.VMEM((256, 2048), bf16)]
        + [pltpu.VMEM((48, 2048), bf16), pltpu.VMEM((128, 2048), bf16)]
        + work_scratch(),
        compiler_params=params(),
        name="second_sweep",
    )(place, applied_current, *pieces, part, state, cell, position, *in_hbm(start, k, w, circuit))
    base, surface_column = pl.pallas_call(
        shell_kernel,
        grid=(8,),
        in_specs=[
            pl.BlockSpec((8, 64, 128), lambda i: (i, 0, 0)),
            pl.BlockSpec((1, 128), lambda i: (0, 0)),
            pl.BlockSpec((64, 128), lambda i: (0, 0)),
        ],
        out_specs=[pl.BlockSpec((8, 128), lambda i: (i, 0))] * 2,
        out_shape=[shape(64, 128)] * 2,
        compiler_params=params(8),
        name="shells",
    )(shell_inverse.reshape(64, 64, 128), shells, conc)
    flux = jnp.sum(lax.all_to_all(flux, "gz", 0, 0, tiled=True), axis=0, keepdims=True)
    updated = base + shell_step * flux * surface_column
    return (concentration, potential, updated[None, None])


def solution(mesh):
    placed = (
        P("gx", "gy", "gz"),
        P("gx", "gy", "gz"),
        P("gx", "gy", "gz"),
        P(),
        P("gx", "gy", "gz"),
        P("gx", "gy", "gz"),
        P("gx", "gy", "gz"),
        P("gx", "gy", "gz"),
        P("gx", "gy", "gz"),
        P("gx", "gy", None),
        P("gx", "gy", "gz"),
        P("gx", "gy", None, "gz"),
        P("gx", "gy", None, None, "gz"),
    )
    return jax.shard_map(
        on_device,
        mesh=mesh,
        in_specs=placed,
        out_specs=(P("gx", "gy", "gz"), P("gx", "gy", "gz"), P("gx", "gy", None, "gz")),
        check_vma=False,
    )
```

```python
import functools

import jax
import jax.numpy as jnp
from jax import lax
from jax.experimental import pallas as pl
from jax.experimental.pallas import tpu as pltpu
from jax.sharding import PartitionSpec as P

SWEEPS = 2
ITERS = 8

inv_step = 4.0
conc_coupling = 0.5
solid_factor = 0.1
shell_step = 0.02

ROWS = 160
FIRST = 16
TILES = 18
PART_ROWS = 2
SUM_ROWS = 16
SETUP = 18
LAST = 16
f32 = jnp.float32
bf16 = jnp.bfloat16
VMEM = pl.BlockSpec(memory_space=pltpu.VMEM)
SMEM = pl.BlockSpec(memory_space=pltpu.SMEM)
HBM = pl.BlockSpec(memory_space=pltpu.HBM)
ANY = pl.BlockSpec(memory_space=pl.ANY)


LONG = pl.CostEstimate(flops=0, bytes_accessed=160 * 1024 * 1024, transcendentals=0)


def params(mebibytes=24):
    return pltpu.CompilerParams(vmem_limit_bytes=mebibytes * 1024 * 1024)


def in_hbm(*arrays):
    return [pltpu.with_memory_space_constraint(array, pltpu.HBM) for array in arrays]


def in_vmem(*arrays):
    return [pltpu.with_memory_space_constraint(array, pltpu.VMEM) for array in arrays]


def copies(sources, targets, sems):
    return [pltpu.make_async_copy(s, t, sems.at[n]) for n, (s, t) in enumerate(zip(sources, targets))]


def iota(shape, dim):
    return lax.broadcasted_iota(jnp.int32, shape, dim)


def lookup(table_ref, rows, low, high, init):
    value = init
    for row in range(rows):
        line = jnp.broadcast_to(table_ref[pl.ds(row, 1), :], (8, 128))
        found = jnp.take_along_axis(line, low, axis=1)
        value = found if row == 0 else jnp.where(high == row, found, value)
    return value


def split_value(value, pieces):
    out = []
    for _ in range(pieces):
        part = value.astype(bf16).astype(f32)
        out.append(part)
        value = value - part
    return out


def by_particle(value, position, left_ref, right_ref):
    parts = split_value(value, 3)
    low = jnp.bitwise_and(position, 127)
    high = jnp.right_shift(position, 7)
    row_high = iota((16, 128), 0)
    row_low = iota((128, 128), 0)
    for t in range(16):
        mask = row_high == high[t : t + 1]
        for n, part in enumerate(parts):
            left_ref[16 * n : 16 * n + 16, 128 * t : 128 * t + 128] = jnp.where(mask, part[t : t + 1], 0.0).astype(bf16)
        right_ref[:, 128 * t : 128 * t + 128] = jnp.where(row_low == low[t : t + 1], 1.0, 0.0).astype(bf16)
    total = lax.dot_general(left_ref[...], right_ref[...], (((1,), (1,)), ((), ())), preferred_element_type=f32)
    return total[0:8] + total[16:24] + total[32:40]


def mark_rows(cell, high_ref):
    high = jnp.right_shift(cell, 7)
    row = iota((256, 128), 0)
    for t in range(16):
        high_ref[:, 128 * t : 128 * t + 128] = jnp.where(row == high[t : t + 1], 1.0, 0.0).astype(bf16)


def sample(flat, cell, high_ref):
    parts = split_value(flat.T, 2)
    left = jnp.concatenate(parts, axis=0).astype(bf16)
    low = jnp.bitwise_and(cell, 127)
    row = iota((128, 128), 0)
    out = []
    for t in range(0, 16, 2):
        found = jnp.dot(left, high_ref[:, 128 * t : 128 * t + 256], preferred_element_type=f32)
        found = found[0:128] + found[128:256]
        for u in range(2):
            mask = row == low[t + u : t + u + 1]
            out.append(jnp.sum(jnp.where(mask, found[:, 128 * u : 128 * u + 128], 0.0), axis=0, keepdims=True))
    return jnp.concatenate(out, axis=0)


def open_circuit(surface_conc):
    return 0.4 * jnp.tanh(3.0 * (0.5 - surface_conc))


def prepare_kernel(
    place_ref,
    count_ref,
    cell_hbm,
    label_hbm,
    owner_hbm,
    area_hbm,
    rate_hbm,
    conc_hbm,
    cond_hbm,
    phase_hbm,
    shells_hbm,
    shell_conc_hbm,
    fields_ref,
    z_first_ref,
    z_second_ref,
    column_ref,
    position_ref,
    owner_f_ref,
    high_ref,
    value_ref,
    left_ref,
    right_ref,
    cell_ref,
    label_ref,
    owner_ref,
    area_ref,
    rate_ref,
    conc_ref,
    cond_ref,
    phase_ref,
    shells_ref,
    shell_conc_ref,
    sems,
):
    held = (cell_ref, label_ref, owner_ref, area_ref, rate_ref, conc_ref, cond_ref, phase_ref, shells_ref, shell_conc_ref)
    given = (cell_hbm, label_hbm, owner_hbm, area_hbm, rate_hbm, conc_hbm, cond_hbm, phase_hbm, shells_hbm, shell_conc_hbm)
    reads = copies(given, held, sems)
    for read in reads:
        read.start()
    for read in reads:
        read.wait()
    lane = iota((16, 128), 1)
    slot = iota((16, 128), 0) * 128 + lane
    live = (slot < count_ref[0, 0, 0]).astype(f32)
    label = label_ref[...]
    owner_f_ref[...] = owner_ref[...].astype(f32)
    low = jnp.bitwise_and(label, 127)
    high = jnp.right_shift(label, 7)
    position = jnp.concatenate(
        [lookup(owner_f_ref, 8, low[h : h + 8], high[h : h + 8], None) for h in (0, 8)], axis=0
    ).astype(jnp.int32)
    position_ref[...] = position
    area = area_ref[...]
    weight = live * area * rate_ref[...]
    cell = cell_ref[...]
    cell_low = jnp.bitwise_and(cell, 127)
    mark_rows(cell, high_ref)

    parts = split_value(weight, 2) + [
        jnp.right_shift(position, 3).astype(f32),
        jnp.bitwise_and(position, 7).astype(f32),
    ]
    row_low = iota((128, 128), 0)
    for t in range(16):
        columns = slice(128 * t, 128 * t + 128)
        mask = row_low == cell_low[t : t + 1]
        for n, part in enumerate(parts):
            value_ref[128 * n : 128 * n + 128, columns] = jnp.where(mask, part[t : t + 1], 0.0).astype(bf16)
    dense = lax.dot_general(high_ref[...], value_ref[...], (((1,), (1,)), ((), ())), preferred_element_type=f32)
    fields_ref[0] = conc_ref[...]
    fields_ref[1] = cond_ref[...] * jnp.where(phase_ref[...] == 1, solid_factor, 1.0)
    fields_ref[2] = (dense[:, 0:128] + dense[:, 128:256]).reshape(16, 16, 128)
    fields_ref[3] = (dense[:, 256:384] * 8.0 + dense[:, 384:512]).reshape(16, 16, 128)

    for f in range(4):
        z_low = jnp.zeros((16, 128), f32)
        z_high = jnp.zeros((16, 128), f32)
        for x in range(16):
            plane = fields_ref[f, x]
            mask = jnp.right_shift(lane, 3) == x
            z_low = jnp.where(mask, pltpu.roll(plane, 8 * x, 1) if x else plane, z_low)
            z_high = jnp.where(mask, pltpu.roll(plane, (8 * x + 8) % 128, 1) if x < 15 else plane, z_high)
        z_first_ref[f], z_second_ref[f] = give(place_ref[6] == 0, z_low, z_high)

    sampled = sample(conc_ref[...].reshape(256, 128), cell, high_ref)
    summed = by_particle(weight * (1.0 + 0.5 * jnp.tanh(sampled)), position, left_ref, right_ref)
    surface_shell = iota((64, 128), 0) == shells_ref[...] - 1
    surface = jnp.sum(jnp.where(surface_shell, shell_conc_ref[...], 0.0), axis=0, keepdims=True)
    area_sum = jnp.sum(live * area, axis=0, keepdims=True)
    tail = jnp.concatenate([surface, area_sum, jnp.zeros((6, 128), f32)], axis=0)
    block = jnp.concatenate([summed, tail], axis=0)
    for n in range(8):
        column_ref[n] = block


def column_kernel(column_ref, sums_ref):
    weight = jnp.zeros((8, 128), f32)
    area = jnp.zeros((1, 128), f32)
    for n in range(8):
        weight = weight + column_ref[n, 0:8]
        area = area + column_ref[n, 9:10]
    surface = jnp.concatenate([column_ref[n, 8:9] for n in range(8)], axis=0)
    circuit = open_circuit(surface)
    growth = jnp.exp(-0.5 * circuit)
    shrink = jnp.exp(0.5 * circuit)
    current = jnp.sum(weight * (growth - shrink), axis=0, keepdims=True)
    slope = jnp.sum(weight * (0.5 * (growth + shrink)), axis=0, keepdims=True)
    block = jnp.concatenate([circuit, current, slope, area, jnp.zeros((5, 128), f32)], axis=0)
    for n in range(sums_ref.shape[0]):
        sums_ref[n, 0:16] = block


def total_of(value):
    return jnp.sum(jnp.sum(value, axis=0, keepdims=True), axis=1, keepdims=True)


def shift(value, by):
    return pltpu.roll(value, by % 128, 1)


def widen(load, wide_ref):
    def square(planes):
        return jnp.concatenate([load(p, t) for p in planes for t in range(4)], axis=0).T

    for n in range(8):
        wide_ref[n, FIRST : FIRST + 128] = square((16 + n, n, 8 + n, 25 + n))
    ends = square((24, 34, 35, 33))
    for n in range(8):
        wide_ref[n, FIRST - 8 : FIRST] = ends[8 * n : 8 * n + 8]
        wide_ref[n, FIRST + 128 : FIRST + 136] = ends[64 + 8 * n : 72 + 8 * n]
        wide_ref[n, 0 : FIRST - 8] = jnp.zeros((8, 128), f32)
        wide_ref[n, FIRST + 136 : ROWS] = jnp.zeros((8, 128), f32)


def loader(f, place_ref, centre_ref, ends_ref, x_first_ref, x_second_ref, y_first_ref, y_second_ref):
    even_x, even_y = place_ref[4] == 0, place_ref[5] == 0

    def load(plane, tile):
        if tile in (0, 3):
            return take(even_y, y_first_ref[f, plane], y_second_ref[f, plane])[tile // 3]
        rows = slice(8 * tile - 8, 8 * tile)
        if plane < 16:
            return centre_ref[f, plane, rows]
        if plane < 34:
            side, n = divmod(plane - 16, 9)
            return take(even_x, x_first_ref[f, n, rows], x_second_ref[f, n, rows])[side]
        return ends_ref[f, plane - 34, rows]

    return load


def narrow(wide_ref, store):
    for n in range(8):
        square = wide_ref[n, FIRST : FIRST + 128].T
        store(n, square[40:56])
        store(8 + n, square[72:88])


def end_slabs(wide_ref):
    square = jnp.concatenate(
        [wide_ref[n, FIRST : FIRST + 8] for n in range(8)]
        + [wide_ref[n, FIRST + 120 : FIRST + 128] for n in range(8)],
        axis=0,
    ).T
    first, second = square[40:56], square[72:88]
    low_half = iota((16, 128), 1) < 64
    low = jnp.where(low_half, first, shift(second, 64))
    high = jnp.where(low_half, shift(first, 64), second)
    return low, high


def tiles(body, first=0, last=TILES, unroll=1):
    def step(n, carry):
        body(pl.multiple_of(8 + 8 * n, 8))
        return carry

    lax.fori_loop(first, last, step, 0, unroll=unroll)


def solve(c_ref, p_ref, start_ref, k_ref, w_ref, circuit_ref, solid, work):
    fx, fy, fz, rc, rp, gc, gp, coup, dc, dp, dc_next, dp_next = work

    def set_faces(r):
        k = [k_ref[n, pl.ds(r, 8)] for n in range(8)]
        for n in range(8):
            below = k[n - 1] if n else shift(k[7], 32)
            fx[n, pl.ds(r, 8)] = 0.5 * (k[n] + below)
            fy[n, pl.ds(r, 8)] = 0.5 * (k[n] + shift(k[n], 1))
            fz[n, pl.ds(r, 8)] = 0.5 * (k[n] + k_ref[n, pl.ds(r - 1, 8)])

    for n in range(8):
        fz[n, FIRST + 136 : ROWS] = jnp.zeros((8, 128), f32)
        for ref in (dc, dp, dc_next, dp_next):
            ref[n, 0 : FIRST - 8] = jnp.zeros((8, 128), f32)
            ref[n, FIRST + 136 : ROWS] = jnp.zeros((8, 128), f32)
    tiles(set_faces, unroll=SETUP)

    def faces(r):
        lower = [fx[n, pl.ds(r, 8)] for n in range(8)]
        return lower + [shift(lower[0], -32)]

    def beside(values, n, source, r, x_faces, y_face, z_face, z_next):
        low = values[n - 1] if n else shift(values[7], 32)
        high = values[n + 1] if n < 7 else shift(values[0], -32)
        total = x_faces[n] * low + x_faces[n + 1] * high
        total = total + (y_face * shift(values[n], 1) + shift(y_face * values[n], -1))
        return total + (z_face * source[n, pl.ds(r - 1, 8)] + z_next * source[n, pl.ds(r + 1, 8)])

    def set_system(r):
        rows = pl.ds(r, 8)
        c = [c_ref[n, rows] for n in range(8)]
        p = None if p_ref is None else [p_ref[n, rows] for n in range(8)]
        x_faces = faces(r)
        for n in range(8):
            y_face, z_face, z_next = fy[n, rows], fz[n, rows], fz[n, pl.ds(r + 1, 8)]
            face_total = x_faces[n] + x_faces[n + 1] + y_face + shift(y_face, -1) + z_face + z_next
            over = solid - circuit_ref[n, rows]
            if p is not None:
                over = over - p[n]
            growth = jnp.exp(0.5 * over)
            shrink = jnp.exp(-0.5 * over)
            factor = w_ref[n, rows] * (1.0 + 0.5 * jnp.tanh(c[n]))
            source = factor * (growth - shrink)
            uptake = factor * (0.5 * (growth + shrink))
            rhs_c = beside(c, n, c_ref, r, x_faces, y_face, z_face, z_next) - face_total * c[n] - conc_coupling * source
            rhs_p = source
            if p is not None:
                rhs_c = rhs_c - (c[n] - start_ref[n, rows]) * inv_step
                rhs_p = rhs_p + (beside(p, n, p_ref, r, x_faces, y_face, z_face, z_next) - face_total * p[n])
            inside = k_ref[n, rows] > 0.0
            recip_c = jnp.where(inside, 1.0 / (inv_step + face_total), 0.0)
            recip_p = jnp.where(inside, 1.0 / (face_total + uptake), 0.0)
            rc[n, rows] = rhs_c
            rp[n, rows] = rhs_p
            gc[n, rows] = recip_c
            gp[n, rows] = recip_p
            coup[n, rows] = conc_coupling * uptake
            dc[n, rows] = rhs_c * recip_c
            dp[n, rows] = rhs_p * recip_p

    tiles(set_system, unroll=SETUP)

    def iteration(c_now, p_now, c_then, p_then, first=0, last=TILES):
        def relax(r):
            rows = pl.ds(r, 8)
            c = [c_now[n, rows] for n in range(8)]
            p = [p_now[n, rows] for n in range(8)]
            x_faces = faces(r)
            for n in range(8):
                y_face, z_face, z_next = fy[n, rows], fz[n, rows], fz[n, pl.ds(r + 1, 8)]
                next_c = beside(c, n, c_now, r, x_faces, y_face, z_face, z_next)
                next_p = beside(p, n, p_now, r, x_faces, y_face, z_face, z_next)
                c_then[n, rows] = (rc[n, rows] + next_c + coup[n, rows] * p[n]) * gc[n, rows]
                p_then[n, rows] = (rp[n, rows] + next_p) * gp[n, rows]

        tiles(relax, first, last, unroll=last - first)

    def pair(_, carry):
        iteration(dc, dp, dc_next, dp_next)
        iteration(dc_next, dp_next, dc, dp)
        return carry

    lax.fori_loop(0, (ITERS - 1) // 2, pair, 0)
    if ITERS % 2 == 0:
        iteration(dc, dp, dc_next, dp_next, 1, TILES - 1)
        return dc_next, dp_next
    return dc, dp


def first_kernel(
    place_ref,
    current_ref,
    centre_ref,
    ends_ref,
    x_first_ref,
    x_second_ref,
    y_first_ref,
    y_second_ref,
    sums_ref,
    start_hbm,
    k_hbm,
    w_hbm,
    circuit_hbm,
    fields_ref,
    z_first_ref,
    z_second_ref,
    part_ref,
    state_ref,
    start_ref,
    k_ref,
    w_ref,
    circuit_ref,
    sems,
    c_ref,
    table_ref,
    *work,
):
    writes = copies((start_ref, k_ref, w_ref, circuit_ref), (start_hbm, k_hbm, w_hbm, circuit_hbm), sems)
    pieces = (place_ref, centre_ref, ends_ref, x_first_ref, x_second_ref, y_first_ref, y_second_ref)
    widen(loader(0, *pieces), start_ref)
    widen(loader(1, *pieces), k_ref)
    widen(loader(2, *pieces), w_ref)
    at_x, at_y, size_x, size_y = place_ref[0], place_ref[1], place_ref[2], place_ref[3]
    for i in range(3):
        for j in range(3):
            near_x = jnp.clip(at_x + (i - 1), 0, size_x - 1)
            near_y = jnp.clip(at_y + (j - 1), 0, size_y - 1)
            table_ref[3 * i + j] = sums_ref[near_x * size_y + near_y, 0:8]
    positions = loader(3, *pieces)

    def circuit(plane, tile):
        i = 0 if 16 <= plane < 25 else 2 if 25 <= plane < 34 else 1
        j = (0, 1, 1, 2)[tile]
        position = positions(plane, tile).astype(jnp.int32)
        return lookup(
            table_ref.at[3 * i + j], 8, jnp.bitwise_and(position, 127), jnp.right_shift(position, 7), None
        )

    widen(circuit, circuit_ref)
    for write in writes:
        write.start()

    sums = sums_ref[0, 8:16]
    for n in range(1, sums_ref.shape[0]):
        sums = sums + sums_ref[n, 8:16]
    sums = jnp.sum(sums, axis=1, keepdims=True)
    current, slope, area = sums[0:1], sums[1:2], sums[2:3]
    solid = (current_ref[0] * area - current) / slope
    dc, dp = solve(start_ref, None, start_ref, k_ref, w_ref, circuit_ref, solid, work)

    lane = iota((8, 128), 1)
    mine = (lane >= 32) & (lane < 96) & (lane % 32 >= 8) & (lane % 32 < 24)
    zero = jnp.zeros((8, 128), f32)

    def finish(n, carry):
        rows = pl.ds(pl.multiple_of(8 + 8 * n, 8), 8)
        total, weight = carry
        for m in range(8):
            c = start_ref[m, rows] + dc[m, rows]
            p = dp[m, rows]
            c_ref[m, rows] = c
            over = solid - p - circuit_ref[m, rows]
            growth = jnp.exp(0.5 * over)
            shrink = jnp.exp(-0.5 * over)
            factor = w_ref[m, rows] * (1.0 + 0.5 * jnp.tanh(c))
            total = total + factor * (growth - shrink)
            weight = weight + factor * (0.5 * (growth + shrink))
        return total, weight

    total, weight = lax.fori_loop(1, TILES - 1, finish, (zero, zero), unroll=LAST)
    total = total_of(jnp.where(mine, total, 0.0))
    weight = total_of(jnp.where(mine, weight, 0.0))
    row = iota((8, 128), 1)
    block = jnp.where(row == 0, total, jnp.where(row == 1, weight, 0.0))

    def spread(n, carry):
        part_ref[n] = block[: part_ref.shape[1]]
        return carry

    lax.fori_loop(0, part_ref.shape[0], spread, 0, unroll=8)
    state_ref[...] = jnp.where(row == 0, solid, jnp.where(row == 1, area, 0.0))
    for f, ref in enumerate((c_ref, dp)):

        def store(plane, value, f=f):
            fields_ref[f, plane] = value

        narrow(ref, store)
        z_first_ref[f], z_second_ref[f] = give(place_ref[6] == 0, *end_slabs(ref))
    for write in writes:
        write.wait()


def second_kernel(
    place_ref,
    current_ref,
    centre_ref,
    ends_ref,
    x_first_ref,
    x_second_ref,
    y_first_ref,
    y_second_ref,
    part_ref,
    state_ref,
    cell_ref,
    position_ref,
    start_hbm,
    k_hbm,
    w_hbm,
    circuit_hbm,
    conc_ref,
    pot_ref,
    flux_ref,
    start_ref,
    k_ref,
    w_ref,
    circuit_ref,
    sems,
    c_ref,
    p_ref,
    flat_ref,
    high_ref,
    left_ref,
    right_ref,
    *work,
):
    pieces = (place_ref, centre_ref, ends_ref, x_first_ref, x_second_ref, y_first_ref, y_second_ref)
    reads = copies((start_hbm, k_hbm, w_hbm, circuit_hbm), (start_ref, k_ref, w_ref, circuit_ref), sems)
    for read in reads:
        read.start()
    widen(loader(0, *pieces), c_ref)
    widen(loader(1, *pieces), p_ref)
    for read in reads:
        read.wait()
    sums = part_ref[0]
    for n in range(1, part_ref.shape[0]):
        sums = sums + part_ref[n]
    sums = sums[0:1]
    current, slope = sums[:, 0:1], sums[:, 1:2]
    before, area = state_ref[0:1, 0:1], state_ref[0:1, 1:2]
    solid = before + (current_ref[0] * area - current) / slope
    dc, dp = solve(c_ref, p_ref, start_ref, k_ref, w_ref, circuit_ref, solid, work)
    flux = work[0]

    def finish(r):
        rows = pl.ds(r, 8)
        for m in range(8):
            c = c_ref[m, rows] + dc[m, rows]
            p = p_ref[m, rows] + dp[m, rows]
            c_ref[m, rows] = c
            p_ref[m, rows] = p
            over = solid - p - circuit_ref[m, rows]
            factor = w_ref[m, rows] * (1.0 + 0.5 * jnp.tanh(c))
            flux[m, rows] = factor * (jnp.exp(0.5 * over) - jnp.exp(-0.5 * over))

    tiles(finish, 1, TILES - 1, unroll=LAST)

    def store_conc(plane, value):
        conc_ref[plane] = value

    def store_pot(plane, value):
        pot_ref[plane] = value

    def store_flux(plane, value):
        flat_ref[16 * plane : 16 * plane + 16] = value

    narrow(flux, store_flux)
    cell = cell_ref[...]
    mark_rows(cell, high_ref)
    sampled = sample(flat_ref[...], cell, high_ref)
    flux_ref[...] = by_particle(sampled, position_ref[...], left_ref, right_ref)
    narrow(c_ref, store_conc)
    narrow(p_ref, store_pot)


def shell_kernel(inverse_ref, shells_ref, conc_ref, base_ref, column_ref):
    count = shells_ref[...]
    index = iota((64, 128), 0)
    fill = (index < count).astype(f32)
    surface = index == count - 1
    load = conc_ref[...] * fill
    rows = inverse_ref.shape[0]
    base, column = [], []
    for i in range(rows):
        matrix = inverse_ref[i]
        base.append(jnp.sum(matrix * load, axis=0, keepdims=True))
        column.append(jnp.sum(jnp.where(surface, matrix, 0.0), axis=0, keepdims=True))
    keep = (iota((rows, 128), 0) + pl.program_id(0) * rows < count).astype(f32)
    base_ref[...] = jnp.concatenate(base, axis=0) * keep
    column_ref[...] = jnp.concatenate(column, axis=0) * keep


def trade(first, second, axis):
    count = lax.axis_size(axis)
    pairs = [(i, i ^ 1) for i in range(count)]
    others = [(i, i + 1) for i in range(1, count - 1, 2)]
    others = others + [(target, source) for source, target in others]
    return lax.ppermute(first, axis, pairs), lax.ppermute(second, axis, others)


def give(even, low, high):
    return jnp.where(even, high, low), jnp.where(even, low, high)


def take(even, first, second):
    return jnp.where(even, second, first), jnp.where(even, first, second)


def pack_x_kernel(place_ref, fields_ref, z_first_ref, z_second_ref, *rest):
    x_first_ref, x_second_ref, ends_ref = rest[-3:]
    even_x, even_z = place_ref[4] == 0, place_ref[6] == 0
    low_half = iota((16, 128), 1) < 64
    for f in range(fields_ref.shape[0]):
        below, above = take(even_z, z_first_ref[f], z_second_ref[f])
        first = jnp.where(low_half, below, shift(above, 64))
        second = jnp.where(low_half, shift(below, 64), above)
        ends_ref[f, 0] = first
        ends_ref[f, 1] = second
        x_first_ref[f, 8], x_second_ref[f, 8] = give(even_x, first, second)
        for n in range(8):
            x_first_ref[f, n], x_second_ref[f, n] = give(even_x, fields_ref[f, n], fields_ref[f, 8 + n])


def pack_y_kernel(place_ref, fields_ref, ends_ref, x_first_ref, x_second_ref, *rest):
    y_first_ref, y_second_ref = rest[-2:]
    even_x, even_y = place_ref[4] == 0, place_ref[5] == 0

    def put(f, plane, value):
        y_first_ref[f, plane], y_second_ref[f, plane] = give(even_y, value[0:8], value[8:16])

    for f in range(fields_ref.shape[0]):
        for n in range(16):
            put(f, n, fields_ref[f, n])
        for n in range(9):
            low, high = take(even_x, x_first_ref[f, n], x_second_ref[f, n])
            put(f, 16 + n, low)
            put(f, 25 + n, high)
        for n in range(2):
            put(f, 34 + n, ends_ref[f, n])


def exchange(place, fields, z_first, z_second, before_x=(), before_y=()):
    count = fields.shape[0]
    z_first, z_second = trade(z_first, z_second, "gz")
    x_first, x_second, ends = pl.pallas_call(
        pack_x_kernel,
        in_specs=[SMEM] + [VMEM] * 3 + [ANY] * len(before_x),
        out_specs=[VMEM] * 3,
        out_shape=[shape(count, 9, 16, 128), shape(count, 9, 16, 128), shape(count, 2, 16, 128)],
        compiler_params=params(8),
        cost_estimate=LONG,
        name="pack_x",
    )(place, fields, z_first, z_second, *before_x)
    x_first, x_second = trade(x_first, x_second, "gx")
    y_first, y_second = pl.pallas_call(
        pack_y_kernel,
        in_specs=[SMEM] + [VMEM] * 4 + [ANY] * len(before_y),
        out_specs=[VMEM] * 2,
        out_shape=[shape(count, 36, 8, 128)] * 2,
        compiler_params=params(8),
        cost_estimate=LONG,
        name="pack_y",
    )(place, fields, ends, x_first, x_second, *before_y)
    y_first, y_second = trade(y_first, y_second, "gy")
    return fields, ends, x_first, x_second, y_first, y_second


def shape(*dims, dtype=f32):
    return jax.ShapeDtypeStruct(dims, dtype)


def wide_scratch(count):
    return [pltpu.VMEM((8, ROWS, 128), f32) for _ in range(count)]


def work_scratch():
    return wide_scratch(12)


def on_device(
    electrolyte,
    conductivity,
    phase_label,
    applied_current,
    slot_count,
    slot_cell,
    slot_label,
    slot_area,
    slot_rate,
    owner_map,
    shell_count,
    shell_conc,
    shell_inverse,
):
    size_x, size_y, size_z = (lax.axis_size(a) for a in ("gx", "gy", "gz"))
    at = [lax.axis_index(a) for a in ("gx", "gy", "gz")]
    place = jnp.stack(at[:2] + [size_x, size_y] + [a % 2 for a in at]).astype(jnp.int32)
    cell = slot_cell.reshape(16, 128)
    shells = shell_count.reshape(1, 128)
    conc = shell_conc.reshape(64, 128)
    given = (
        cell,
        slot_label.reshape(16, 128),
        owner_map.reshape(8, 128),
        slot_area.reshape(16, 128),
        slot_rate.reshape(16, 128),
        electrolyte,
        conductivity,
        phase_label,
        shells,
        conc,
    )
    fields, z_first, z_second, column, position = pl.pallas_call(
        prepare_kernel,
        in_specs=[SMEM] * 2 + [HBM] * 10,
        out_specs=[VMEM] * 5,
        out_shape=[
            shape(4, 16, 16, 128),
            shape(4, 16, 128),
            shape(4, 16, 128),
            shape(8, 16, 128),
            shape(16, 128, dtype=jnp.int32),
        ],
        scratch_shapes=[
            pltpu.VMEM((8, 128), f32),
            pltpu.VMEM((256, 2048), bf16),
            pltpu.VMEM((512, 2048), bf16),
            pltpu.VMEM((48, 2048), bf16),
            pltpu.VMEM((128, 2048), bf16),
        ]
        + [pltpu.VMEM(array.shape, array.dtype) for array in given]
        + [pltpu.SemaphoreType.DMA((len(given),))],
        compiler_params=params(12),
        name="prepare",
    )(place, slot_count, *in_hbm(*given))
    column = lax.all_to_all(column, "gz", 0, 0, tiled=True)
    sums = pl.pallas_call(
        column_kernel,
        in_specs=[VMEM],
        out_specs=VMEM,
        out_shape=shape(size_x * size_y, SUM_ROWS, 128),
        compiler_params=params(4),
        name="column",
    )(column)
    pieces = exchange(place, fields, z_first, z_second, (column,), (sums,))
    sums = lax.all_to_all(sums, ("gx", "gy"), 0, 0, tiled=True)
    wide = shape(8, ROWS, 128)
    devices = size_x * size_y * size_z
    start, k, w, circuit, fields, z_first, z_second, part, state = pl.pallas_call(
        first_kernel,
        in_specs=[SMEM] * 2 + [VMEM] * 7,
        out_specs=[HBM] * 4 + [VMEM] * 5,
        out_shape=[
            *[pltpu.HBM(wide.shape, f32)] * 4,
            shape(2, 16, 16, 128),
            shape(2, 16, 128),
            shape(2, 16, 128),
            shape(devices, PART_ROWS, 128),
            shape(8, 128),
        ],
        scratch_shapes=wide_scratch(4)
        + [pltpu.SemaphoreType.DMA((4,))]
        + wide_scratch(1)
        + [pltpu.VMEM((9, 8, 128), f32)]
        + work_scratch(),
        compiler_params=params(),
        name="first_sweep",
    )(place, applied_current, *pieces, sums)
    pieces = exchange(place, fields, z_first, z_second)
    part = lax.all_to_all(part, ("gx", "gy", "gz"), 0, 0, tiled=True)
    concentration, potential, flux = pl.pallas_call(
        second_kernel,
        in_specs=[SMEM] * 2 + [VMEM] * 10 + [HBM] * 4,
        out_specs=[VMEM] * 3,
        out_shape=[shape(16, 16, 128), shape(16, 16, 128), shape(8, 128)],
        scratch_shapes=wide_scratch(4)
        + [pltpu.SemaphoreType.DMA((4,))]
        + wide_scratch(2)
        + [pltpu.VMEM((256, 128), f32), pltpu.VMEM((256, 2048), bf16)]
        + [pltpu.VMEM((48, 2048), bf16), pltpu.VMEM((128, 2048), bf16)]
        + work_scratch(),
        compiler_params=params(),
        name="second_sweep",
    )(place, applied_current, *in_vmem(*pieces), part, state, cell, position, *in_hbm(start, k, w, circuit))
    base, surface_column = pl.pallas_call(
        shell_kernel,
        grid=(8,),
        in_specs=[
            pl.BlockSpec((8, 64, 128), lambda i: (i, 0, 0)),
            pl.BlockSpec((1, 128), lambda i: (0, 0)),
            pl.BlockSpec((64, 128), lambda i: (0, 0)),
        ],
        out_specs=[pl.BlockSpec((8, 128), lambda i: (i, 0))] * 2,
        out_shape=[shape(64, 128)] * 2,
        compiler_params=params(8),
        name="shells",
    )(shell_inverse.reshape(64, 64, 128), shells, conc)
    flux = jnp.sum(lax.all_to_all(flux, "gz", 0, 0, tiled=True), axis=0, keepdims=True)
    updated = base + shell_step * flux * surface_column
    return (concentration, potential, updated[None, None])


def solution(mesh):
    placed = (
        P("gx", "gy", "gz"),
        P("gx", "gy", "gz"),
        P("gx", "gy", "gz"),
        P(),
        P("gx", "gy", "gz"),
        P("gx", "gy", "gz"),
        P("gx", "gy", "gz"),
        P("gx", "gy", "gz"),
        P("gx", "gy", "gz"),
        P("gx", "gy", None),
        P("gx", "gy", "gz"),
        P("gx", "gy", None, "gz"),
        P("gx", "gy", None, None, "gz"),
    )
    return jax.shard_map(
        on_device,
        mesh=mesh,
        in_specs=placed,
        out_specs=(P("gx", "gy", "gz"), P("gx", "gy", "gz"), P("gx", "gy", None, "gz")),
        check_vma=False,
    )
```

```python
import functools

import jax
import jax.numpy as jnp
from jax import lax
from jax.experimental import pallas as pl
from jax.experimental.pallas import tpu as pltpu
from jax.sharding import PartitionSpec as P

SWEEPS = 2
ITERS = 8

inv_step = 4.0
conc_coupling = 0.5
solid_factor = 0.1
shell_step = 0.02

ROWS = 160
FIRST = 16
TILES = 18
PART_ROWS = 2
SUM_ROWS = 16
SETUP = 18
LAST = 16
f32 = jnp.float32
bf16 = jnp.bfloat16
VMEM = pl.BlockSpec(memory_space=pltpu.VMEM)
SMEM = pl.BlockSpec(memory_space=pltpu.SMEM)
HBM = pl.BlockSpec(memory_space=pltpu.HBM)
ANY = pl.BlockSpec(memory_space=pl.ANY)


LONG = pl.CostEstimate(flops=0, bytes_accessed=160 * 1024 * 1024, transcendentals=0)


def params(mebibytes=24):
    return pltpu.CompilerParams(vmem_limit_bytes=mebibytes * 1024 * 1024)


def in_hbm(*arrays):
    return [pltpu.with_memory_space_constraint(array, pltpu.HBM) for array in arrays]


def in_vmem(*arrays):
    return [pltpu.with_memory_space_constraint(array, pltpu.VMEM) for array in arrays]


def copies(sources, targets, sems):
    return [pltpu.make_async_copy(s, t, sems.at[n]) for n, (s, t) in enumerate(zip(sources, targets))]


def iota(shape, dim):
    return lax.broadcasted_iota(jnp.int32, shape, dim)


def lookup(table_ref, rows, low, high, init):
    value = init
    for row in range(rows):
        line = jnp.broadcast_to(table_ref[pl.ds(row, 1), :], (8, 128))
        found = jnp.take_along_axis(line, low, axis=1)
        value = found if row == 0 else jnp.where(high == row, found, value)
    return value


def split_value(value, pieces):
    out = []
    for _ in range(pieces):
        part = value.astype(bf16).astype(f32)
        out.append(part)
        value = value - part
    return out


def by_particle(value, position, left_ref, right_ref):
    parts = split_value(value, 3)
    low = jnp.bitwise_and(position, 127)
    high = jnp.right_shift(position, 7)
    row_high = iota((16, 128), 0)
    row_low = iota((128, 128), 0)
    for t in range(16):
        mask = row_high == high[t : t + 1]
        for n, part in enumerate(parts):
            left_ref[16 * n : 16 * n + 16, 128 * t : 128 * t + 128] = jnp.where(mask, part[t : t + 1], 0.0).astype(bf16)
        right_ref[:, 128 * t : 128 * t + 128] = jnp.where(row_low == low[t : t + 1], 1.0, 0.0).astype(bf16)
    total = lax.dot_general(left_ref[...], right_ref[...], (((1,), (1,)), ((), ())), preferred_element_type=f32)
    return total[0:8] + total[16:24] + total[32:40]


def mark_rows(cell, high_ref):
    high = jnp.right_shift(cell, 7)
    row = iota((256, 128), 0)
    for t in range(16):
        high_ref[:, 128 * t : 128 * t + 128] = jnp.where(row == high[t : t + 1], 1.0, 0.0).astype(bf16)


def sample(flat, cell, high_ref):
    parts = split_value(flat.T, 2)
    left = jnp.concatenate(parts, axis=0).astype(bf16)
    low = jnp.bitwise_and(cell, 127)
    row = iota((128, 128), 0)
    out = []
    for t in range(0, 16, 2):
        found = jnp.dot(left, high_ref[:, 128 * t : 128 * t + 256], preferred_element_type=f32)
        found = found[0:128] + found[128:256]
        for u in range(2):
            mask = row == low[t + u : t + u + 1]
            out.append(jnp.sum(jnp.where(mask, found[:, 128 * u : 128 * u + 128], 0.0), axis=0, keepdims=True))
    return jnp.concatenate(out, axis=0)


def open_circuit(surface_conc):
    return 0.4 * jnp.tanh(3.0 * (0.5 - surface_conc))


def prepare_kernel(
    place_ref,
    count_ref,
    cell_hbm,
    label_hbm,
    owner_hbm,
    area_hbm,
    rate_hbm,
    conc_hbm,
    cond_hbm,
    phase_hbm,
    shells_hbm,
    shell_conc_hbm,
    fields_ref,
    z_first_ref,
    z_second_ref,
    column_ref,
    position_ref,
    owner_f_ref,
    high_ref,
    value_ref,
    left_ref,
    right_ref,
    cell_ref,
    label_ref,
    owner_ref,
    area_ref,
    rate_ref,
    conc_ref,
    cond_ref,
    phase_ref,
    shells_ref,
    shell_conc_ref,
    sems,
):
    held = (cell_ref, label_ref, owner_ref, area_ref, rate_ref, conc_ref, cond_ref, phase_ref, shells_ref, shell_conc_ref)
    given = (cell_hbm, label_hbm, owner_hbm, area_hbm, rate_hbm, conc_hbm, cond_hbm, phase_hbm, shells_hbm, shell_conc_hbm)
    reads = copies(given, held, sems)
    for read in reads:
        read.start()
    for read in reads:
        read.wait()
    lane = iota((16, 128), 1)
    slot = iota((16, 128), 0) * 128 + lane
    live = (slot < count_ref[0, 0, 0]).astype(f32)
    label = label_ref[...]
    owner_f_ref[...] = owner_ref[...].astype(f32)
    low = jnp.bitwise_and(label, 127)
    high = jnp.right_shift(label, 7)
    position = jnp.concatenate(
        [lookup(owner_f_ref, 8, low[h : h + 8], high[h : h + 8], None) for h in (0, 8)], axis=0
    ).astype(jnp.int32)
    position_ref[...] = position
    area = area_ref[...]
    weight = live * area * rate_ref[...]
    cell = cell_ref[...]
    cell_low = jnp.bitwise_and(cell, 127)
    mark_rows(cell, high_ref)

    parts = split_value(weight, 2) + [
        jnp.right_shift(position, 3).astype(f32),
        jnp.bitwise_and(position, 7).astype(f32),
    ]
    row_low = iota((128, 128), 0)
    for t in range(16):
        columns = slice(128 * t, 128 * t + 128)
        mask = row_low == cell_low[t : t + 1]
        for n, part in enumerate(parts):
            value_ref[128 * n : 128 * n + 128, columns] = jnp.where(mask, part[t : t + 1], 0.0).astype(bf16)
    dense = lax.dot_general(high_ref[...], value_ref[...], (((1,), (1,)), ((), ())), preferred_element_type=f32)
    fields_ref[0] = conc_ref[...]
    fields_ref[1] = cond_ref[...] * jnp.where(phase_ref[...] == 1, solid_factor, 1.0)
    fields_ref[2] = (dense[:, 0:128] + dense[:, 128:256]).reshape(16, 16, 128)
    fields_ref[3] = (dense[:, 256:384] * 8.0 + dense[:, 384:512]).reshape(16, 16, 128)

    for f in range(4):
        z_low = jnp.zeros((16, 128), f32)
        z_high = jnp.zeros((16, 128), f32)
        for x in range(16):
            plane = fields_ref[f, x]
            mask = jnp.right_shift(lane, 3) == x
            z_low = jnp.where(mask, pltpu.roll(plane, 8 * x, 1) if x else plane, z_low)
            z_high = jnp.where(mask, pltpu.roll(plane, (8 * x + 8) % 128, 1) if x < 15 else plane, z_high)
        z_first_ref[f], z_second_ref[f] = give(place_ref[6] == 0, z_low, z_high)

    sampled = sample(conc_ref[...].reshape(256, 128), cell, high_ref)
    summed = by_particle(weight * (1.0 + 0.5 * jnp.tanh(sampled)), position, left_ref, right_ref)
    surface_shell = iota((64, 128), 0) == shells_ref[...] - 1
    surface = jnp.sum(jnp.where(surface_shell, shell_conc_ref[...], 0.0), axis=0, keepdims=True)
    area_sum = jnp.sum(live * area, axis=0, keepdims=True)
    tail = jnp.concatenate([surface, area_sum, jnp.zeros((6, 128), f32)], axis=0)
    block = jnp.concatenate([summed, tail], axis=0)
    for n in range(8):
        column_ref[n] = block


def column_kernel(column_ref, sums_ref):
    weight = jnp.zeros((8, 128), f32)
    area = jnp.zeros((1, 128), f32)
    for n in range(8):
        weight = weight + column_ref[n, 0:8]
        area = area + column_ref[n, 9:10]
    surface = jnp.concatenate([column_ref[n, 8:9] for n in range(8)], axis=0)
    circuit = open_circuit(surface)
    growth = jnp.exp(-0.5 * circuit)
    shrink = jnp.exp(0.5 * circuit)
    current = jnp.sum(weight * (growth - shrink), axis=0, keepdims=True)
    slope = jnp.sum(weight * (0.5 * (growth + shrink)), axis=0, keepdims=True)
    block = jnp.concatenate([circuit, current, slope, area, jnp.zeros((5, 128), f32)], axis=0)
    for n in range(sums_ref.shape[0]):
        sums_ref[n, 0:16] = block


def total_of(value):
    return jnp.sum(jnp.sum(value, axis=0, keepdims=True), axis=1, keepdims=True)


def shift(value, by):
    return pltpu.roll(value, by % 128, 1)


def widen(load, wide_ref):
    def square(planes):
        return jnp.concatenate([load(p, t) for p in planes for t in range(4)], axis=0).T

    for n in range(8):
        wide_ref[n, FIRST : FIRST + 128] = square((16 + n, n, 8 + n, 25 + n))
    ends = square((24, 34, 35, 33))
    for n in range(8):
        wide_ref[n, FIRST - 8 : FIRST] = ends[8 * n : 8 * n + 8]
        wide_ref[n, FIRST + 128 : FIRST + 136] = ends[64 + 8 * n : 72 + 8 * n]
        wide_ref[n, 0 : FIRST - 8] = jnp.zeros((8, 128), f32)
        wide_ref[n, FIRST + 136 : ROWS] = jnp.zeros((8, 128), f32)


def loader(f, place_ref, centre_ref, ends_ref, x_first_ref, x_second_ref, y_first_ref, y_second_ref):
    even_x, even_y = place_ref[4] == 0, place_ref[5] == 0

    def load(plane, tile):
        if tile in (0, 3):
            return take(even_y, y_first_ref[f, plane], y_second_ref[f, plane])[tile // 3]
        rows = slice(8 * tile - 8, 8 * tile)
        if plane < 16:
            return centre_ref[f, plane, rows]
        if plane < 34:
            side, n = divmod(plane - 16, 9)
            return take(even_x, x_first_ref[f, n, rows], x_second_ref[f, n, rows])[side]
        return ends_ref[f, plane - 34, rows]

    return load


def narrow(wide_ref, store):
    for n in range(8):
        square = wide_ref[n, FIRST : FIRST + 128].T
        store(n, square[40:56])
        store(8 + n, square[72:88])


def end_slabs(wide_ref):
    square = jnp.concatenate(
        [wide_ref[n, FIRST : FIRST + 8] for n in range(8)]
        + [wide_ref[n, FIRST + 120 : FIRST + 128] for n in range(8)],
        axis=0,
    ).T
    first, second = square[40:56], square[72:88]
    low_half = iota((16, 128), 1) < 64
    low = jnp.where(low_half, first, shift(second, 64))
    high = jnp.where(low_half, shift(first, 64), second)
    return low, high


def tiles(body, first=0, last=TILES, unroll=1):
    def step(n, carry):
        body(pl.multiple_of(8 + 8 * n, 8))
        return carry

    lax.fori_loop(first, last, step, 0, unroll=unroll)


def solve(c_ref, p_ref, start_ref, k_ref, w_ref, circuit_ref, solid, work):
    fx, fy, fz, rc, rp, gc, gp, coup, dc, dp, dc_next, dp_next = work

    def set_faces(r):
        k = [k_ref[n, pl.ds(r, 8)] for n in range(8)]
        for n in range(8):
            below = k[n - 1] if n else shift(k[7], 32)
            fx[n, pl.ds(r, 8)] = 0.5 * (k[n] + below)
            fy[n, pl.ds(r, 8)] = 0.5 * (k[n] + shift(k[n], 1))
            fz[n, pl.ds(r, 8)] = 0.5 * (k[n] + k_ref[n, pl.ds(r - 1, 8)])

    for n in range(8):
        fz[n, FIRST + 136 : ROWS] = jnp.zeros((8, 128), f32)
        for ref in (dc, dp, dc_next, dp_next):
            ref[n, 0 : FIRST - 8] = jnp.zeros((8, 128), f32)
            ref[n, FIRST + 136 : ROWS] = jnp.zeros((8, 128), f32)
    tiles(set_faces, unroll=SETUP)

    def faces(r):
        lower = [fx[n, pl.ds(r, 8)] for n in range(8)]
        return lower + [shift(lower[0], -32)]

    def beside(values, n, source, r, x_faces, y_face, z_face, z_next):
        low = values[n - 1] if n else shift(values[7], 32)
        high = values[n + 1] if n < 7 else shift(values[0], -32)
        total = x_faces[n] * low + x_faces[n + 1] * high
        total = total + (y_face * shift(values[n], 1) + shift(y_face * values[n], -1))
        return total + (z_face * source[n, pl.ds(r - 1, 8)] + z_next * source[n, pl.ds(r + 1, 8)])

    def set_system(r):
        rows = pl.ds(r, 8)
        c = [c_ref[n, rows] for n in range(8)]
        p = None if p_ref is None else [p_ref[n, rows] for n in range(8)]
        x_faces = faces(r)
        for n in range(8):
            y_face, z_face, z_next = fy[n, rows], fz[n, rows], fz[n, pl.ds(r + 1, 8)]
            face_total = x_faces[n] + x_faces[n + 1] + y_face + shift(y_face, -1) + z_face + z_next
            over = solid - circuit_ref[n, rows]
            if p is not None:
                over = over - p[n]
            growth = jnp.exp(0.5 * over)
            shrink = jnp.exp(-0.5 * over)
            factor = w_ref[n, rows] * (1.0 + 0.5 * jnp.tanh(c[n]))
            source = factor * (growth - shrink)
            uptake = factor * (0.5 * (growth + shrink))
            rhs_c = beside(c, n, c_ref, r, x_faces, y_face, z_face, z_next) - face_total * c[n] - conc_coupling * source
            rhs_p = source
            if p is not None:
                rhs_c = rhs_c - (c[n] - start_ref[n, rows]) * inv_step
                rhs_p = rhs_p + (beside(p, n, p_ref, r, x_faces, y_face, z_face, z_next) - face_total * p[n])
            inside = k_ref[n, rows] > 0.0
            recip_c = jnp.where(inside, 1.0 / (inv_step + face_total), 0.0)
            recip_p = jnp.where(inside, 1.0 / (face_total + uptake), 0.0)
            rc[n, rows] = rhs_c
            rp[n, rows] = rhs_p
            gc[n, rows] = recip_c
            gp[n, rows] = recip_p
            coup[n, rows] = conc_coupling * uptake
            dc[n, rows] = rhs_c * recip_c
            dp[n, rows] = rhs_p * recip_p

    tiles(set_system, unroll=SETUP)

    def iteration(c_now, p_now, c_then, p_then, first=0, last=TILES):
        def relax(r):
            rows = pl.ds(r, 8)
            c = [c_now[n, rows] for n in range(8)]
            p = [p_now[n, rows] for n in range(8)]
            x_faces = faces(r)
            for n in range(8):
                y_face, z_face, z_next = fy[n, rows], fz[n, rows], fz[n, pl.ds(r + 1, 8)]
                next_c = beside(c, n, c_now, r, x_faces, y_face, z_face, z_next)
                next_p = beside(p, n, p_now, r, x_faces, y_face, z_face, z_next)
                c_then[n, rows] = (rc[n, rows] + next_c + coup[n, rows] * p[n]) * gc[n, rows]
                p_then[n, rows] = (rp[n, rows] + next_p) * gp[n, rows]

        tiles(relax, first, last, unroll=last - first)

    def pair(_, carry):
        iteration(dc, dp, dc_next, dp_next)
        iteration(dc_next, dp_next, dc, dp)
        return carry

    lax.fori_loop(0, (ITERS - 1) // 2, pair, 0)
    if ITERS % 2 == 0:
        iteration(dc, dp, dc_next, dp_next, 1, TILES - 1)
        return dc_next, dp_next
    return dc, dp


def first_kernel(
    place_ref,
    current_ref,
    centre_ref,
    ends_ref,
    x_first_ref,
    x_second_ref,
    y_first_ref,
    y_second_ref,
    sums_ref,
    start_hbm,
    k_hbm,
    w_hbm,
    circuit_hbm,
    fields_ref,
    z_first_ref,
    z_second_ref,
    part_ref,
    state_ref,
    start_ref,
    k_ref,
    w_ref,
    circuit_ref,
    sems,
    c_ref,
    table_ref,
    *work,
):
    writes = copies((start_ref, k_ref, w_ref, circuit_ref), (start_hbm, k_hbm, w_hbm, circuit_hbm), sems)
    pieces = (place_ref, centre_ref, ends_ref, x_first_ref, x_second_ref, y_first_ref, y_second_ref)
    widen(loader(0, *pieces), start_ref)
    widen(loader(1, *pieces), k_ref)
    widen(loader(2, *pieces), w_ref)
    at_x, at_y, size_x, size_y = place_ref[0], place_ref[1], place_ref[2], place_ref[3]
    for i in range(3):
        for j in range(3):
            near_x = jnp.clip(at_x + (i - 1), 0, size_x - 1)
            near_y = jnp.clip(at_y + (j - 1), 0, size_y - 1)
            table_ref[3 * i + j] = sums_ref[near_x * size_y + near_y, 0:8]
    positions = loader(3, *pieces)

    def circuit(plane, tile):
        i = 0 if 16 <= plane < 25 else 2 if 25 <= plane < 34 else 1
        j = (0, 1, 1, 2)[tile]
        position = positions(plane, tile).astype(jnp.int32)
        return lookup(
            table_ref.at[3 * i + j], 8, jnp.bitwise_and(position, 127), jnp.right_shift(position, 7), None
        )

    widen(circuit, circuit_ref)
    for write in writes:
        write.start()

    sums = sums_ref[0, 8:16]
    for n in range(1, sums_ref.shape[0]):
        sums = sums + sums_ref[n, 8:16]
    sums = jnp.sum(sums, axis=1, keepdims=True)
    current, slope, area = sums[0:1], sums[1:2], sums[2:3]
    solid = (current_ref[0] * area - current) / slope
    dc, dp = solve(start_ref, None, start_ref, k_ref, w_ref, circuit_ref, solid, work)

    lane = iota((8, 128), 1)
    mine = (lane >= 32) & (lane < 96) & (lane % 32 >= 8) & (lane % 32 < 24)
    zero = jnp.zeros((8, 128), f32)

    def finish(n, carry):
        rows = pl.ds(pl.multiple_of(8 + 8 * n, 8), 8)
        total, weight = carry
        for m in range(8):
            c = start_ref[m, rows] + dc[m, rows]
            p = dp[m, rows]
            c_ref[m, rows] = c
            over = solid - p - circuit_ref[m, rows]
            growth = jnp.exp(0.5 * over)
            shrink = jnp.exp(-0.5 * over)
            factor = w_ref[m, rows] * (1.0 + 0.5 * jnp.tanh(c))
            total = total + factor * (growth - shrink)
            weight = weight + factor * (0.5 * (growth + shrink))
        return total, weight

    total, weight = lax.fori_loop(1, TILES - 1, finish, (zero, zero), unroll=LAST)
    total = total_of(jnp.where(mine, total, 0.0))
    weight = total_of(jnp.where(mine, weight, 0.0))
    row = iota((8, 128), 1)
    block = jnp.where(row == 0, total, jnp.where(row == 1, weight, 0.0))

    def spread(n, carry):
        part_ref[n] = block[: part_ref.shape[1]]
        return carry

    lax.fori_loop(0, part_ref.shape[0], spread, 0, unroll=8)
    state_ref[...] = jnp.where(row == 0, solid, jnp.where(row == 1, area, 0.0))
    for f, ref in enumerate((c_ref, dp)):

        def store(plane, value, f=f):
            fields_ref[f, plane] = value

        narrow(ref, store)
        z_first_ref[f], z_second_ref[f] = give(place_ref[6] == 0, *end_slabs(ref))
    for write in writes:
        write.wait()


def second_kernel(
    place_ref,
    current_ref,
    centre_ref,
    ends_ref,
    x_first_ref,
    x_second_ref,
    y_first_ref,
    y_second_ref,
    part_ref,
    state_ref,
    cell_ref,
    position_ref,
    start_hbm,
    k_hbm,
    w_hbm,
    circuit_hbm,
    conc_ref,
    pot_ref,
    flux_ref,
    start_ref,
    k_ref,
    w_ref,
    circuit_ref,
    sems,
    c_ref,
    p_ref,
    flat_ref,
    high_ref,
    left_ref,
    right_ref,
    *work,
):
    pieces = (place_ref, centre_ref, ends_ref, x_first_ref, x_second_ref, y_first_ref, y_second_ref)
    reads = copies((start_hbm, k_hbm, w_hbm, circuit_hbm), (start_ref, k_ref, w_ref, circuit_ref), sems)
    for read in reads:
        read.start()
    widen(loader(0, *pieces), c_ref)
    widen(loader(1, *pieces), p_ref)
    for read in reads:
        read.wait()
    sums = part_ref[0]
    for n in range(1, part_ref.shape[0]):
        sums = sums + part_ref[n]
    sums = sums[0:1]
    current, slope = sums[:, 0:1], sums[:, 1:2]
    before, area = state_ref[0:1, 0:1], state_ref[0:1, 1:2]
    solid = before + (current_ref[0] * area - current) / slope
    dc, dp = solve(c_ref, p_ref, start_ref, k_ref, w_ref, circuit_ref, solid, work)
    flux = work[0]

    def finish(r):
        rows = pl.ds(r, 8)
        for m in range(8):
            c = c_ref[m, rows] + dc[m, rows]
            p = p_ref[m, rows] + dp[m, rows]
            c_ref[m, rows] = c
            p_ref[m, rows] = p
            over = solid - p - circuit_ref[m, rows]
            factor = w_ref[m, rows] * (1.0 + 0.5 * jnp.tanh(c))
            flux[m, rows] = factor * (jnp.exp(0.5 * over) - jnp.exp(-0.5 * over))

    tiles(finish, 1, TILES - 1, unroll=LAST)

    def store_conc(plane, value):
        conc_ref[plane] = value

    def store_pot(plane, value):
        pot_ref[plane] = value

    def store_flux(plane, value):
        flat_ref[16 * plane : 16 * plane + 16] = value

    narrow(flux, store_flux)
    cell = cell_ref[...]
    mark_rows(cell, high_ref)
    sampled = sample(flat_ref[...], cell, high_ref)
    flux_ref[...] = by_particle(sampled, position_ref[...], left_ref, right_ref)
    narrow(c_ref, store_conc)
    narrow(p_ref, store_pot)


def shell_kernel(inverse_ref, shells_ref, conc_ref, base_ref, column_ref):
    count = shells_ref[...]
    index = iota((64, 128), 0)
    fill = (index < count).astype(f32)
    surface = index == count - 1
    load = conc_ref[...] * fill
    rows = inverse_ref.shape[0]
    base, column = [], []
    for i in range(rows):
        matrix = inverse_ref[i]
        base.append(jnp.sum(matrix * load, axis=0, keepdims=True))
        column.append(jnp.sum(jnp.where(surface, matrix, 0.0), axis=0, keepdims=True))
    keep = (iota((rows, 128), 0) + pl.program_id(0) * rows < count).astype(f32)
    base_ref[...] = jnp.concatenate(base, axis=0) * keep
    column_ref[...] = jnp.concatenate(column, axis=0) * keep


def trade(first, second, axis):
    count = lax.axis_size(axis)
    pairs = [(i, i ^ 1) for i in range(count)]
    others = [(i, i + 1) for i in range(1, count - 1, 2)]
    others = others + [(target, source) for source, target in others]
    return lax.ppermute(first, axis, pairs), lax.ppermute(second, axis, others)


def give(even, low, high):
    return jnp.where(even, high, low), jnp.where(even, low, high)


def take(even, first, second):
    return jnp.where(even, second, first), jnp.where(even, first, second)


def pack_x_kernel(place_ref, fields_ref, z_first_ref, z_second_ref, *rest):
    x_first_ref, x_second_ref, ends_ref = rest[-3:]
    even_x, even_z = place_ref[4] == 0, place_ref[6] == 0
    low_half = iota((16, 128), 1) < 64
    for f in range(fields_ref.shape[0]):
        below, above = take(even_z, z_first_ref[f], z_second_ref[f])
        first = jnp.where(low_half, below, shift(above, 64))
        second = jnp.where(low_half, shift(below, 64), above)
        ends_ref[f, 0] = first
        ends_ref[f, 1] = second
        x_first_ref[f, 8], x_second_ref[f, 8] = give(even_x, first, second)
        for n in range(8):
            x_first_ref[f, n], x_second_ref[f, n] = give(even_x, fields_ref[f, n], fields_ref[f, 8 + n])


def pack_y_kernel(place_ref, fields_ref, ends_ref, x_first_ref, x_second_ref, *rest):
    y_first_ref, y_second_ref = rest[-2:]
    even_x, even_y = place_ref[4] == 0, place_ref[5] == 0

    def put(f, plane, value):
        y_first_ref[f, plane], y_second_ref[f, plane] = give(even_y, value[0:8], value[8:16])

    for f in range(fields_ref.shape[0]):
        for n in range(16):
            put(f, n, fields_ref[f, n])
        for n in range(9):
            low, high = take(even_x, x_first_ref[f, n], x_second_ref[f, n])
            put(f, 16 + n, low)
            put(f, 25 + n, high)
        for n in range(2):
            put(f, 34 + n, ends_ref[f, n])


def exchange(place, fields, z_first, z_second, before_x=(), before_y=()):
    count = fields.shape[0]
    z_first, z_second = trade(z_first, z_second, "gz")
    x_first, x_second, ends = pl.pallas_call(
        pack_x_kernel,
        in_specs=[SMEM] + [VMEM] * 3 + [ANY] * len(before_x),
        out_specs=[VMEM] * 3,
        out_shape=[shape(count, 9, 16, 128), shape(count, 9, 16, 128), shape(count, 2, 16, 128)],
        compiler_params=params(8),
        cost_estimate=LONG,
        name="pack_x",
    )(place, fields, z_first, z_second, *before_x)
    x_first, x_second = trade(x_first, x_second, "gx")
    y_first, y_second = pl.pallas_call(
        pack_y_kernel,
        in_specs=[SMEM] + [VMEM] * 4 + [ANY] * len(before_y),
        out_specs=[VMEM] * 2,
        out_shape=[shape(count, 36, 8, 128)] * 2,
        compiler_params=params(8),
        cost_estimate=LONG,
        name="pack_y",
    )(place, fields, ends, x_first, x_second, *before_y)
    y_first, y_second = trade(y_first, y_second, "gy")
    return fields, ends, x_first, x_second, y_first, y_second


def shape(*dims, dtype=f32):
    return jax.ShapeDtypeStruct(dims, dtype)


def wide_scratch(count):
    return [pltpu.VMEM((8, ROWS, 128), f32) for _ in range(count)]


def work_scratch():
    return wide_scratch(12)


def on_device(
    electrolyte,
    conductivity,
    phase_label,
    applied_current,
    slot_count,
    slot_cell,
    slot_label,
    slot_area,
    slot_rate,
    owner_map,
    shell_count,
    shell_conc,
    shell_inverse,
):
    size_x, size_y, size_z = (lax.axis_size(a) for a in ("gx", "gy", "gz"))
    at = [lax.axis_index(a) for a in ("gx", "gy", "gz")]
    place = jnp.stack(at[:2] + [size_x, size_y] + [a % 2 for a in at]).astype(jnp.int32)
    cell = slot_cell.reshape(16, 128)
    shells = shell_count.reshape(1, 128)
    conc = shell_conc.reshape(64, 128)
    given = (
        cell,
        slot_label.reshape(16, 128),
        owner_map.reshape(8, 128),
        slot_area.reshape(16, 128),
        slot_rate.reshape(16, 128),
        electrolyte,
        conductivity,
        phase_label,
        shells,
        conc,
    )
    fields, z_first, z_second, column, position = pl.pallas_call(
        prepare_kernel,
        in_specs=[SMEM] * 2 + [HBM] * 10,
        out_specs=[VMEM] * 5,
        out_shape=[
            shape(4, 16, 16, 128),
            shape(4, 16, 128),
            shape(4, 16, 128),
            shape(8, 16, 128),
            shape(16, 128, dtype=jnp.int32),
        ],
        scratch_shapes=[
            pltpu.VMEM((8, 128), f32),
            pltpu.VMEM((256, 2048), bf16),
            pltpu.VMEM((512, 2048), bf16),
            pltpu.VMEM((48, 2048), bf16),
            pltpu.VMEM((128, 2048), bf16),
        ]
        + [pltpu.VMEM(array.shape, array.dtype) for array in given]
        + [pltpu.SemaphoreType.DMA((len(given),))],
        compiler_params=params(12),
        name="prepare",
    )(place, slot_count, *in_hbm(*given))
    column = lax.all_to_all(column, "gz", 0, 0, tiled=True)
    sums = pl.pallas_call(
        column_kernel,
        in_specs=[VMEM],
        out_specs=VMEM,
        out_shape=shape(size_x * size_y, SUM_ROWS, 128),
        compiler_params=params(4),
        name="column",
    )(column)
    pieces = exchange(place, fields, z_first, z_second, (column,), (sums,))
    sums = lax.all_to_all(sums, ("gx", "gy"), 0, 0, tiled=True)
    wide = shape(8, ROWS, 128)
    devices = size_x * size_y * size_z
    start, k, w, circuit, fields, z_first, z_second, part, state = pl.pallas_call(
        first_kernel,
        in_specs=[SMEM] * 2 + [VMEM] * 7,
        out_specs=[HBM] * 4 + [VMEM] * 5,
        out_shape=[
            *[pltpu.HBM(wide.shape, f32)] * 4,
            shape(2, 16, 16, 128),
            shape(2, 16, 128),
            shape(2, 16, 128),
            shape(devices, PART_ROWS, 128),
            shape(8, 128),
        ],
        scratch_shapes=wide_scratch(4)
        + [pltpu.SemaphoreType.DMA((4,))]
        + wide_scratch(1)
        + [pltpu.VMEM((9, 8, 128), f32)]
        + work_scratch(),
        compiler_params=params(),
        name="first_sweep",
    )(place, applied_current, *pieces, sums)
    pieces = exchange(place, fields, z_first, z_second)
    part = lax.all_to_all(part, ("gx", "gy", "gz"), 0, 0, tiled=True)
    concentration, potential, flux = pl.pallas_call(
        second_kernel,
        in_specs=[SMEM] * 2 + [VMEM] * 10 + [HBM] * 4,
        out_specs=[VMEM] * 3,
        out_shape=[shape(16, 16, 128), shape(16, 16, 128), shape(8, 128)],
        scratch_shapes=wide_scratch(4)
        + [pltpu.SemaphoreType.DMA((4,))]
        + wide_scratch(2)
        + [pltpu.VMEM((256, 128), f32), pltpu.VMEM((256, 2048), bf16)]
        + [pltpu.VMEM((48, 2048), bf16), pltpu.VMEM((128, 2048), bf16)]
        + work_scratch(),
        compiler_params=params(),
        name="second_sweep",
    )(place, applied_current, *in_vmem(*pieces), part, state, cell, position, *in_hbm(start, k, w, circuit))
    base, surface_column = pl.pallas_call(
        shell_kernel,
        grid=(8,),
        in_specs=[
            pl.BlockSpec((8, 64, 128), lambda i: (i, 0, 0)),
            pl.BlockSpec((1, 128), lambda i: (0, 0)),
            pl.BlockSpec((64, 128), lambda i: (0, 0)),
        ],
        out_specs=[pl.BlockSpec((8, 128), lambda i: (i, 0))] * 2,
        out_shape=[shape(64, 128)] * 2,
        compiler_params=params(8),
        name="shells",
    )(*in_hbm(shell_inverse.reshape(64, 64, 128)), shells, conc)
    flux = jnp.sum(lax.all_to_all(flux, "gz", 0, 0, tiled=True), axis=0, keepdims=True)
    updated = base + shell_step * flux * surface_column
    return (concentration, potential, updated[None, None])


def solution(mesh):
    placed = (
        P("gx", "gy", "gz"),
        P("gx", "gy", "gz"),
        P("gx", "gy", "gz"),
        P(),
        P("gx", "gy", "gz"),
        P("gx", "gy", "gz"),
        P("gx", "gy", "gz"),
        P("gx", "gy", "gz"),
        P("gx", "gy", "gz"),
        P("gx", "gy", None),
        P("gx", "gy", "gz"),
        P("gx", "gy", None, "gz"),
        P("gx", "gy", None, None, "gz"),
    )
    return jax.shard_map(
        on_device,
        mesh=mesh,
        in_specs=placed,
        out_specs=(P("gx", "gy", "gz"), P("gx", "gy", "gz"), P("gx", "gy", None, "gz")),
        check_vma=False,
    )
```
